32 devices in a mesh: seq: 8 (over z, x), dp: 4 (over y, core).
Axes of the slice: x: 2, y: 2, z: 4, core: 2. Of those that a mesh axis runs over, the one named last changes fastest.
Arguments:
- tokens: bfloat16 [4, 4096, 4096], P('dp', 'seq'), may hold values from -6 to 6
- w_in: bfloat16 [4096, 2336], P(('seq', 'dp')), may hold values from -0.09375 to 0.09375
- conv_w: float32 [4, 2304], replicated, may hold values from -3 to 3
- a_rate: float32 [32], replicated, may hold values from 1.2207031e-05 to 0.06
- d_skip: float32 [32], replicated, may hold values from 0.5 to 2
- level_w: int32 [4, 11], P('dp'), may hold values from 0 to 256
- lengths: int32 [4], P('dp'), may hold values from 64 to 4096, as said below
Outputs:
- mixed_out: bfloat16 [4, 4096, 2048], P('dp', 'seq')
The draws below stay inside these ranges and needn't reach their ends.
Inputs may be any that keep to these rules, and one draw needn't show every extreme that they name: `lengths`: every length is a multiple of 64, and some request has all 4096 positions live.
All inputs are finite; a program needn't handle non-finite values.
Results may differ from the reference program's by a relative error of at most 0.015.
Values may be sent and summed in bfloat16 or wider, within the bound.
A program may use at most 128 MiB of HBM per device.

```python
import math
from functools import partial
import jax
import jax.numpy as jnp
import numpy as np
from jax import lax

D = 4096
HEADS = 32
HEAD_DIM = 64
STATE = 128
Q = 64
CONV = 4
LEVELS = 11
CHANNELS = 2304
PROJ = 2336
LENGTH = 4096
REQUESTS = 4


def draw_lengths(key, part):
    stretch_count = jax.random.randint(key, (REQUESTS,), 1, LENGTH // Q + 1)
    chosen = jax.random.randint(jax.random.fold_in(key, 7), (), 0, REQUESTS)
    stretch_count = jnp.where(jnp.arange(REQUESTS) == chosen, LENGTH // Q, stretch_count)
    return (stretch_count * Q).astype(jnp.int32)


def plant(values, own_key, smallest, top_value):
    spot = [jax.random.randint(jax.random.fold_in(own_key, axis), (), 0, length) for axis, length in enumerate(values.shape)]
    main_axis = values.shape.index(max(values.shape))
    neighbour = spot[:main_axis] + [(spot[main_axis] + 1) % values.shape[main_axis]] + spot[main_axis + 1:]
    return values.at[tuple(spot)].set(smallest).at[tuple(neighbour)].set(top_value)


def block_scale(key, extent, shards, least, high):
    def one(axis_at, shards_of):
        steps = jax.random.uniform(jax.random.fold_in(jax.random.fold_in(key, 6), axis_at), (shards_of,), jnp.float32, least / len(shards), high / len(shards))
        return jnp.repeat(jnp.exp(steps), extent[axis_at] // shards_of).reshape((-1,) + (1,) * (len(extent) - axis_at - 1))

    loudness = one(*shards[0])
    for cut in shards[1:]:
        loudness = loudness * one(*cut)
    return loudness


def bell_draw(own_key, extent, deviation, reach, pieces=(), kind=jnp.bfloat16):
    loudness = block_scale(own_key, extent, pieces, -0.22, 0.18) if pieces else 1.0
    drawn = jax.random.normal(own_key, extent, jnp.float32) * deviation * loudness
    return jnp.minimum(jnp.maximum(drawn, -reach), reach).astype(kind)


def setup_inputs(seed: int = 0) -> dict:
    splits = jax.random.split(jax.random.key(seed), 8)
    return {
        "tokens": bell_draw(splits[0], (REQUESTS, LENGTH, D), 1.0, 6.0, ((0, 4), (1, 8))),
        "w_in": bell_draw(splits[1], (D, PROJ), D ** -0.5, 0.09375, ((0, 32),)),
        "conv_w": bell_draw(splits[2], (CONV, CHANNELS), 0.5, 3.0, (), jnp.float32),
        "a_rate": jnp.clip(jnp.exp(jax.random.uniform(splits[3], (HEADS,), jnp.float32, math.log(1.220703143189894e-05), math.log(0.06))), 1.220703143189894e-05, 0.06),
        "d_skip": jnp.clip(jnp.exp(jax.random.uniform(splits[4], (HEADS,), jnp.float32, math.log(0.5), math.log(2.0))), 0.5, 2.0),
        "level_w": plant(jax.random.randint(splits[5], (REQUESTS, LEVELS), 0, 257), jax.random.fold_in(splits[5], 1), 0, 256).astype(jnp.int32),
        "lengths": draw_lengths(jax.random.fold_in(splits[7], 71), 0),
    }


def level_table(count):
    table = np.zeros((count, count), np.int32)
    for later in range(count):
        for earlier in range(later):
            table[later, earlier] = (earlier ^ later).bit_length()
    return table

def one_request(operands, w_in, conv_w, a_rate, d_skip):
    token_rows, level_row, length = operands
    count = token_rows.shape[0]
    channels = conv_w.shape[1]
    inner = channels - 2 * STATE
    projected = jnp.dot(token_rows, w_in, preferred_element_type=jnp.float32)
    raw = projected[:, :channels].astype(jnp.bfloat16)
    padded = jnp.concatenate([jnp.zeros((CONV - 1, channels), jnp.bfloat16), raw], 0)
    convolved = jnp.zeros((count, channels), jnp.float32)
    for offset in range(CONV):
        convolved = convolved + padded[offset:offset + count].astype(jnp.float32) * conv_w[offset]
    values = jax.nn.silu(convolved[:, :inner]).astype(jnp.bfloat16)
    in_b = convolved[:, inner:inner + STATE].astype(jnp.bfloat16)
    out_c = convolved[:, inner + STATE:].astype(jnp.bfloat16)
    step_size = jax.nn.softplus(projected[:, channels:])
    log_decay = -step_size * a_rate[None, :]
    driven = (values.astype(jnp.float32).reshape(count, HEADS, HEAD_DIM) * step_size[:, :, None]).astype(jnp.bfloat16)
    stretches = count // Q
    cumul = jnp.cumsum(log_decay.reshape(stretches, Q, HEADS), axis=1)
    totals = cumul[:, -1]
    before = jnp.cumsum(totals, axis=0) - totals
    level_wt = level_row.astype(jnp.float32) / 256.0
    keys_b = in_b.reshape(stretches, Q, STATE).astype(jnp.float32)
    query_c = out_c.reshape(stretches, Q, STATE).astype(jnp.float32)
    drive_c = driven.reshape(stretches, Q, HEADS, HEAD_DIM).astype(jnp.float32)
    scores = jnp.einsum('ctn,csn->cts', query_c, keys_b)
    causal = jnp.asarray(np.tril(np.ones((Q, Q), bool)))[None, :, :, None]
    differ = cumul[:, :, None, :] - cumul[:, None, :, :]
    inner_wt = jnp.where(causal, jnp.exp(jnp.where(causal, differ, 0.0)), 0.0) * scores[..., None] * level_wt[0]
    inner_wt = inner_wt.astype(jnp.bfloat16)
    y_inner = jnp.einsum('ctsh,cshp->cthp', inner_wt.astype(jnp.float32), drive_c)
    to_end = jnp.exp(totals[:, None, :] - cumul)
    weighted_b = (keys_b[:, :, None, :] * to_end[..., None]).astype(jnp.bfloat16)
    states = jnp.einsum('cshn,cshp->chnp', weighted_b.astype(jnp.float32), drive_c)
    table = jnp.asarray(level_table(stretches))
    lower = jnp.asarray(np.tril(np.ones((stretches, stretches), bool), -1))[:, :, None]
    spacing = before[:, None, :] - before[None, :, :] - totals[None, :, :]
    mixing = jnp.where(lower, jnp.exp(jnp.where(lower, spacing, 0.0)), 0.0) * level_wt[table][:, :, None]
    carried = jnp.einsum('jih,ihnp->jhnp', mixing, states, precision=lax.Precision.HIGHEST)
    carried_low = carried.astype(jnp.bfloat16).astype(jnp.float32)
    y_cross = jnp.exp(cumul)[..., None] * jnp.einsum('ctn,chnp->cthp', query_c, carried_low)
    output = y_inner + y_cross + d_skip[None, None, :, None] * values.astype(jnp.float32).reshape(stretches, Q, HEADS, HEAD_DIM)
    output = output * lax.rsqrt(lax.optimization_barrier(jnp.mean(output * output, axis=-1, keepdims=True)) + 1e-05)
    position = jnp.arange(count, dtype=jnp.int32).reshape(stretches, Q)
    output = jnp.where((position < length)[:, :, None, None], output, 0.0)
    return output.reshape(count, inner).astype(jnp.bfloat16)

def reference(tokens, w_in, conv_w, a_rate, d_skip, level_w, lengths):
    worker = partial(one_request, w_in=w_in, conv_w=conv_w, a_rate=a_rate, d_skip=d_skip)
    return lax.map(worker, (tokens, level_w, lengths))
```

```python
import functools

import jax
import jax.numpy as jnp
from jax import lax
from jax.experimental import pallas as pl
from jax.experimental.pallas import tpu as pltpu
from jax.sharding import PartitionSpec as P

STATE = 128
Q = 64
RIM = 16
LANES = 128
WIDE = 512
HEAD = 64
MESH = pl.DeviceIdType.MESH
F32 = jnp.float32
BF16 = jnp.bfloat16


def dot(a, b):
    return jnp.dot(a, b, preferred_element_type=F32)


def chunk_list(inner, padded):
    chunks = [(inner, padded - inner)]
    chunks += [(at, WIDE) for at in range(0, inner, WIDE)]
    return chunks


def project_kernel(
    nz, n, inner, tok_ref, w_ref, raw_ref, step_ref, ext, wbuf, tok_sem, rim_sem, own_sem, send_sem, recv_sem, core_send, core_recv
):
    seq = lax.axis_index("seq")
    dp = lax.axis_index("dp")
    nseq = nz * n
    z, x = seq // n, seq % n
    y, core = dp // 2, dp % 2
    rows = w_ref.shape[0]
    count = tok_ref.shape[0]
    padded = w_ref.shape[1]
    chunks = chunk_list(inner, padded)
    after = (seq + 1) % nseq
    prior = (seq + nseq - 1) % nseq

    def place(dz, da, db):
        dx = da * (1 - core) + db * core
        dy = da * core + db * (1 - core)
        return ((z + dz) % nz) * n + (x + dx) % n, ((y + dy) % n) * 2 + core

    def rows_of(device):
        at = device[0] * (2 * n) + device[1]
        return pl.ds(pl.multiple_of(at * rows, rows), rows)

    offsets = [(dz, da, db) for dz in range(nz) for da in range(n) for db in range(n)]
    peers = [(dz, 0, 0) for dz in range(1, nz)]
    peers += [(0, da, 0) for da in range(1, n)] + [(0, 0, db) for db in range(1, n)]
    other = (seq, y * 2 + 1 - core)

    barrier = pltpu.get_barrier_semaphore()
    greeted = [place(*peer) for peer in peers] + [other, (after, dp), (prior, dp)]
    for device in greeted:
        pl.semaphore_signal(barrier, inc=1, device_id=device, device_id_type=MESH)
    pl.semaphore_wait(barrier, len(greeted))

    rim = pltpu.make_async_remote_copy(
        src_ref=tok_ref.at[pl.ds(count - RIM, RIM)],
        dst_ref=ext.at[pl.ds(0, RIM)],
        send_sem=rim_sem.at[0],
        recv_sem=rim_sem.at[1],
        device_id=(after, dp),
        device_id_type=MESH,
    )
    own_rows = rows_of((seq, dp))
    number = {offset: at for at, offset in enumerate(offsets)}
    sends = []

    def link_copy(c, offset, step):
        at, width = chunks[c]
        cols = pl.ds(at, width)
        where = rows_of(place(*offset))
        mine = offset == (0, 0, 0)
        lands = tuple((o - s) % m for o, s, m in zip(offset, step, (nz, n, n)))
        slot = number[lands]
        return pltpu.make_async_remote_copy(
            src_ref=w_ref.at[:, cols] if mine else wbuf.at[where, cols],
            dst_ref=wbuf.at[where, cols],
            send_sem=send_sem.at[c, slot],
            recv_sem=recv_sem.at[c, slot],
            device_id=place(*step),
            device_id_type=MESH,
        )

    def arrived(c, offset):
        at, width = chunks[c]
        ref = wbuf.at[rows_of(place(*offset)), pl.ds(at, width)]
        pltpu.make_async_copy(ref, ref, recv_sem.at[c, number[offset]]).wait()

    def core_copy(c, offset):
        at, width = chunks[c]
        cols = pl.ds(at, width)
        where = rows_of(place(*offset))
        mine = offset == (0, 0, 0)
        return pltpu.make_async_remote_copy(
            src_ref=w_ref.at[:, cols] if mine else wbuf.at[where, cols],
            dst_ref=wbuf.at[where, cols],
            send_sem=core_send.at[c, number[offset]],
            recv_sem=core_recv.at[c, number[offset]],
            device_id=other,
            device_id_type=MESH,
        )

    def core_arrived(c, offset):
        dz, da, db = offset
        at, width = chunks[c]
        theirs = 1 - core
        dx = da * (1 - theirs) + db * theirs
        dy = da * theirs + db * (1 - theirs)
        device = ((z + dz) % nz) * n + (x + dx) % n, ((y + dy) % n) * 2 + theirs
        ref = wbuf.at[rows_of(device), pl.ds(at, width)]
        pltpu.make_async_copy(ref, ref, core_recv.at[c, number[offset]]).wait()

    def start(copy):
        copy.start()
        sends.append(copy)

    def send_on(c, offset):
        if offset[1] == 0 and offset[2] == 0:
            for da in range(1, n):
                start(link_copy(c, offset, (0, da, 0)))
        if offset[2] == 0:
            for db in range(1, n):
                start(link_copy(c, offset, (0, 0, db)))
        start(core_copy(c, offset))

    def send_own(c):
        for dz in range(1, nz):
            start(link_copy(c, (0, 0, 0), (dz, 0, 0)))
        send_on(c, (0, 0, 0))

    def forward(c):
        order = sorted(offsets[1:], key=lambda o: (o[2] > 0, o[1] > 0))
        for offset in order:
            arrived(c, offset)
            send_on(c, offset)

    def multiply(c):
        for offset in offsets:
            core_arrived(c, offset)
        at, width = chunks[c]
        if at < inner:

            @pl.loop(0, width // 256)
            def _(tile):
                cols = pl.ds(pl.multiple_of(at + tile * 256, 256), 256)
                raw_ref[:, cols] = dot(ext[...], wbuf[:, cols]).astype(BF16)

        else:
            mid = at + 2 * STATE
            raw_ref[:, at:mid] = dot(ext[...], wbuf[:, at:mid]).astype(BF16)
            step_ref[...] = dot(ext[...], wbuf[:, mid:])

    send_own(0)
    rim.start()
    tokens_in = pltpu.make_async_copy(tok_ref, ext.at[pl.ds(RIM, count)], tok_sem.at[0])
    tokens_in.start()
    own_in = pltpu.make_async_copy(w_ref, wbuf.at[own_rows], own_sem.at[0])
    own_in.start()
    send_own(1)
    rim.wait()
    tokens_in.wait()
    own_in.wait()

    @pl.when(seq == 0)
    def _():
        ext[0:RIM, :] = jnp.zeros((RIM, ext.shape[1]), BF16)

    for c in range(len(chunks)):
        forward(c)
        if c + 2 < len(chunks):
            send_own(c + 2)
        if c > 0:
            multiply(c - 1)
    multiply(len(chunks) - 1)
    for copy in sends:
        copy.wait_send()


def project(tokens, w_in, inner, nseq, ndp):
    count, depth = tokens.shape
    rows, width = w_in.shape
    padded = -(-width // LANES) * LANES
    n = ndp // 2
    nz = nseq // n
    w_in = jnp.pad(w_in, ((0, 0), (0, padded - width)))
    channels = inner + 2 * STATE
    if nseq * ndp > 32:
        before = lax.ppermute(tokens[count - RIM :], "seq", [(i, i + 1) for i in range(nseq - 1)])
        full = lax.all_gather(w_in, ("seq", "dp"), axis=0, tiled=True)
        out = jnp.dot(jnp.concatenate([before, tokens], 0), full, preferred_element_type=F32)
        return out[:, :channels].astype(BF16), out[:, channels:]
    total = count + RIM
    shards = nz * n * n
    chunks = len(chunk_list(inner, padded))
    return pl.pallas_call(
        functools.partial(project_kernel, nz, n, inner),
        out_shape=(
            jax.ShapeDtypeStruct((total, channels), BF16),
            jax.ShapeDtypeStruct((total, padded - channels), F32),
        ),
        in_specs=[pl.BlockSpec(memory_space=pl.ANY)] * 2,
        out_specs=(pl.BlockSpec(memory_space=pltpu.VMEM),) * 2,
        scratch_shapes=[
            pltpu.VMEM((total, depth), BF16),
            pltpu.VMEM((depth, padded), BF16),
            pltpu.SemaphoreType.DMA((1,)),
            pltpu.SemaphoreType.DMA((2,)),
            pltpu.SemaphoreType.DMA((1,)),
            pltpu.SemaphoreType.DMA((chunks, shards)),
            pltpu.SemaphoreType.DMA((chunks, shards)),
            pltpu.SemaphoreType.DMA((chunks, shards)),
            pltpu.SemaphoreType.DMA((chunks, shards)),
        ],
        compiler_params=pltpu.CompilerParams(
            collective_id=0, has_side_effects=True, vmem_limit_bytes=48 * 2**20
        ),
        name="project",
    )(tokens, w_in)


def split_terms(value, terms):
    parts = []
    for _ in range(terms):
        part = value.astype(BF16)
        parts.append(part)
        value = value - part.astype(F32)
    return parts


def expander(chunk, terms):
    head = lax.broadcasted_iota(jnp.int32, (LANES, WIDE), 0)
    lane = lax.broadcasted_iota(jnp.int32, (LANES, WIDE), 1)
    heads = WIDE // HEAD
    one = jnp.where(head == chunk * heads + lane // HEAD, 1.0, 0.0).astype(BF16)
    return jnp.concatenate([one] * terms, 0)


def expand(value, chunk, terms=2):
    return dot(jnp.concatenate(split_terms(value, terms), 1), expander(chunk, terms))


def convolve(raw, conv_ref, padded_ref, count):
    padded_ref[...] = raw.astype(F32)
    total = jnp.zeros((count, raw.shape[1]), F32)
    for tap in range(4):
        total = total + padded_ref[pl.ds(RIM - 3 + tap, count), :] * conv_ref[tap : tap + 1, :]
    return total


def mix_kernel(
    level_ref, raw_ref, bc_ref, step_ref, conv_ref, conv_bc_ref, rate_ref, skip_ref,
    y_ref, state_ref, sums_ref, reach_ref, query_ref,
    keys_t, cumul_s, cumul_t, scores_s, ends_s, steps_s, padded_s, padded_bc, totals_s,
):
    chunk = pl.program_id(0)
    count = y_ref.shape[0]
    stretches = count // Q
    pairs = count // LANES
    row = lax.broadcasted_iota(jnp.int32, (LANES, LANES), 0)
    col = lax.broadcasted_iota(jnp.int32, (LANES, LANES), 1)
    causal = (col <= row) & (row // Q == col // Q)

    def level(at):
        return level_ref[0, at].astype(F32) / 256.0

    @pl.when(chunk == 0)
    def _():
        both = convolve(bc_ref[...], conv_bc_ref, padded_bc, count)
        keys = both[:, :STATE].astype(BF16)
        query = both[:, STATE:].astype(BF16)
        query_ref[...] = query
        steps = step_ref[pl.ds(RIM, count), :]
        steps = jnp.maximum(steps, 0.0) + jnp.log1p(jnp.exp(-jnp.abs(steps)))
        steps_s[...] = steps
        decay = -steps * rate_ref[...]
        ones = jnp.where(causal, 1.0, 0.0).astype(BF16)
        before = jnp.zeros((1, LANES), F32)
        totals_s[...] = jnp.zeros_like(totals_s)
        for p in range(pairs):
            rows = slice(p * LANES, (p + 1) * LANES)
            terms = split_terms(decay[rows], 3)
            cumul = dot(ones, terms[2]) + dot(ones, terms[1]) + dot(ones, terms[0])
            cumul_s[rows, :] = cumul
            cumul_t[:, rows] = cumul.T
            keys_p = keys[rows].astype(F32).T.astype(BF16)
            keys_t[:, rows] = keys_p
            scores_s[rows, :] = dot(query[rows], keys_p) * level(0)
            for half in range(2):
                part = cumul[half * Q : (half + 1) * Q]
                total = part[Q - 1 : Q]
                at = slice(p * LANES + half * Q, p * LANES + (half + 1) * Q)
                ends_s[at, :] = jnp.exp(total - part)
                reach_ref[at, :] = jnp.exp(part + before)
                totals_s[2 * p + half : 2 * p + half + 1, :] = total
                before = before + total
        sums_ref[...] = jnp.broadcast_to(before, sums_ref.shape)

    convolved = convolve(raw_ref[...], conv_ref, padded_s, count)
    values = (convolved / (1.0 + jnp.exp(-convolved))).astype(BF16).astype(F32)
    driven_f = values * expand(steps_s[...], chunk, 3)
    driven = driven_f.astype(BF16)
    ended = (driven.astype(F32) * expand(ends_s[...], chunk)).astype(BF16)
    totals = expand(totals_s[...], chunk, 3)
    heads = WIDE // HEAD
    turn = (LANES - chunk * heads) % LANES
    left = lax.broadcasted_iota(jnp.int32, (LANES, LANES), 1) < HEAD
    upper = lax.broadcasted_iota(jnp.int32, (LANES, WIDE), 0) < Q
    states = []
    for p in range(pairs):
        rows = slice(p * LANES, (p + 1) * LANES)
        down = pltpu.roll(cumul_s[rows, :], turn, 1)
        along = cumul_t[pl.ds(pl.multiple_of(chunk * heads, heads), heads), rows]
        scores = scores_s[rows, :]
        for two in range(heads // 2):
            cols = slice(two * LANES, (two + 1) * LANES)
            parts = []
            for h in (2 * two, 2 * two + 1):
                differ = down[:, h : h + 1] - along[h : h + 1, :]
                weight = jnp.exp(jnp.where(causal, differ, -1e30)) * scores
                parts.append(dot(weight.astype(BF16), driven[rows, cols]))
            y_ref[rows, cols] = (
                jnp.where(left, parts[0], parts[1]) + skip_ref[:, cols] * values[rows, cols]
            )
        ended_p = ended[rows]
        keys_p = keys_t[:, rows]
        zero = jnp.zeros_like(ended_p)
        states.append(dot(keys_p, jnp.where(upper, ended_p, zero)))
        states.append(dot(keys_p, jnp.where(upper, zero, ended_p)))

    sums = [totals[i : i + 1] for i in range(stretches)]
    carried = [None] * stretches
    blocks, block_sums = states, sums
    bits = stretches.bit_length() - 1
    for bit in range(bits):
        weight = level(bit + 1)
        for k in range(1, len(blocks), 2):
            passed = jnp.zeros((1, WIDE), F32)
            for j in range(k << bit, (k + 1) << bit):
                term = blocks[k - 1] * (weight * jnp.exp(passed))
                carried[j] = term if carried[j] is None else carried[j] + term
                passed = passed + sums[j]
        merged = [
            blocks[k] * jnp.exp(block_sums[k + 1]) + blocks[k + 1] for k in range(0, len(blocks), 2)
        ]
        block_sums = [block_sums[k] + block_sums[k + 1] for k in range(0, len(blocks), 2)]
        blocks = merged
    state_ref[...] = blocks[0].astype(BF16)
    for j in range(1, stretches):
        rows = slice(j * Q, (j + 1) * Q)
        grown = expand(jnp.exp(cumul_s[rows, :]), chunk)
        y_ref[rows, :] += grown * dot(query_ref[rows, :], carried[j].astype(BF16))


def mix(raw, steps, conv_w, rate, skip, level_w, count):
    inner = conv_w.shape[1] - 2 * STATE
    total = raw.shape[0]
    whole = lambda shape: pl.BlockSpec(shape, lambda i: (0, 0))
    part = lambda rows: pl.BlockSpec((rows, WIDE), lambda i: (0, i))
    tail = lambda rows: pl.BlockSpec((rows, 2 * STATE), lambda i: (0, inner // (2 * STATE)))
    return pl.pallas_call(
        mix_kernel,
        grid=(inner // WIDE,),
        in_specs=[
            pl.BlockSpec(memory_space=pltpu.SMEM),
            part(total),
            tail(total),
            whole((total, LANES)),
            part(4),
            tail(4),
            whole((1, LANES)),
            part(1),
        ],
        out_specs=(part(count), part(STATE), whole((8, LANES)), whole((count, LANES)), whole((count, STATE))),
        out_shape=(
            jax.ShapeDtypeStruct((count, inner), F32),
            jax.ShapeDtypeStruct((STATE, inner), BF16),
            jax.ShapeDtypeStruct((8, LANES), F32),
            jax.ShapeDtypeStruct((count, LANES), F32),
            jax.ShapeDtypeStruct((count, STATE), BF16),
        ),
        scratch_shapes=[
            pltpu.VMEM((STATE, count), BF16),
            pltpu.VMEM((count, LANES), F32),
            pltpu.VMEM((LANES, count), F32),
            pltpu.VMEM((count, LANES), F32),
            pltpu.VMEM((count, LANES), F32),
            pltpu.VMEM((count, LANES), F32),
            pltpu.VMEM((total, WIDE), F32),
            pltpu.VMEM((total, 2 * STATE), F32),
            pltpu.VMEM((max(8, count // Q), LANES), F32),
        ],
        compiler_params=pltpu.CompilerParams(vmem_limit_bytes=48 * 2**20),
        name="mix",
    )(level_w, raw, raw, steps, conv_w, conv_w, rate, skip)


def finish_kernel(live_ref, y_ref, cross_ref, reach_ref, query_ref, out_ref):
    chunk = pl.program_id(0)
    count = y_ref.shape[0]
    output = y_ref[...] + expand(reach_ref[...], chunk) * dot(query_ref[...], cross_ref[...])
    squares = output * output
    row = lax.broadcasted_iota(jnp.int32, (LANES, LANES), 0)
    col = lax.broadcasted_iota(jnp.int32, (LANES, LANES), 1)
    same = jnp.where(row // HEAD == col // HEAD, 1.0 / HEAD, 0.0).astype(BF16)
    same = jnp.concatenate([same, same], 0)
    places = lax.broadcasted_iota(jnp.int32, (count, LANES), 0)
    live = places < live_ref[0]
    for two in range(WIDE // LANES):
        cols = slice(two * LANES, (two + 1) * LANES)
        mean = dot(jnp.concatenate(split_terms(squares[:, cols], 2), 1), same)
        out_ref[:, cols] = jnp.where(live, output[:, cols] * lax.rsqrt(mean + 1e-05), 0.0).astype(BF16)


def finish(live, y, cross, reach, query):
    count, inner = y.shape
    whole = lambda shape: pl.BlockSpec(shape, lambda i: (0, 0))
    part = lambda rows: pl.BlockSpec((rows, WIDE), lambda i: (0, i))
    return pl.pallas_call(
        finish_kernel,
        grid=(inner // WIDE,),
        in_specs=[
            pl.BlockSpec(memory_space=pltpu.SMEM),
            part(count),
            part(STATE),
            whole((count, LANES)),
            whole((count, STATE)),
        ],
        out_specs=part(count),
        out_shape=jax.ShapeDtypeStruct((count, inner), BF16),
        compiler_params=pltpu.CompilerParams(vmem_limit_bytes=48 * 2**20),
        name="finish",
    )(live, y, cross, reach, query)


def swapped(value, axis, stride):
    mask = 2**stride
    pairs = [(source, source ^ mask) for source in range(lax.axis_size(axis))]
    return lax.ppermute(value, axis, pairs)


def body(tokens, w_in, conv_w, a_rate, d_skip, level_w, lengths):
    token_rows = tokens.reshape(-1, tokens.shape[-1])
    count = token_rows.shape[0]
    heads = a_rate.shape[0]
    inner = conv_w.shape[1] - 2 * STATE
    nseq = lax.axis_size("seq")
    raw, steps = project(token_rows, w_in, inner, nseq, lax.axis_size("dp"))
    rate = jnp.pad(a_rate[None, :], ((0, 0), (0, LANES - heads)))
    skip = jnp.repeat(d_skip, HEAD)[None, :]
    y, block_state, sums, reach, query = mix(raw, steps, conv_w, rate, skip, level_w, count)
    level_wt = level_w.reshape(-1).astype(F32) / 256.0
    position = lax.axis_index("seq")
    wide = lambda value: jnp.repeat(value, HEAD)[None, :]
    block_state = block_state.astype(F32)
    block_total = sums[0, :heads]
    cross_state = jnp.zeros_like(block_state)
    passed = jnp.zeros_like(block_total)
    local_bits = (count // Q).bit_length() - 1
    for level in range(nseq.bit_length() - 1):
        other_state = swapped(block_state.astype(BF16), "seq", level).astype(F32)
        other_total = swapped(block_total, "seq", level)
        upper = (jnp.right_shift(position, level) & 1).astype(F32)
        weight = upper * level_wt[local_bits + level + 1]
        cross_state = cross_state + weight * wide(jnp.exp(passed)) * other_state
        passed = passed + upper * other_total
        block_state = jnp.where(
            upper > 0.5,
            other_state * wide(jnp.exp(block_total)) + block_state,
            block_state * wide(jnp.exp(other_total)) + other_state,
        )
        block_total = block_total + other_total
    live = lengths - position * count
    out = finish(live, y, cross_state.astype(BF16), reach, query)
    return out.reshape(1, count, inner)


def solution(mesh):
    in_specs = (P("dp", "seq", None), P(("seq", "dp"), None), P(), P(), P(), P("dp", None), P("dp"))
    out_specs = P("dp", "seq", None)
    return jax.shard_map(body, mesh=mesh, in_specs=in_specs, out_specs=out_specs, check_vma=False)
```

```python
import functools

import jax
import jax.numpy as jnp
from jax import lax
from jax.experimental import pallas as pl
from jax.experimental.pallas import tpu as pltpu
from jax.sharding import PartitionSpec as P

STATE = 128
Q = 64
RIM = 16
LANES = 128
WIDE = 512
HEAD = 64
MESH = pl.DeviceIdType.MESH
F32 = jnp.float32
BF16 = jnp.bfloat16


def dot(a, b):
    return jnp.dot(a, b, preferred_element_type=F32)


def chunk_list(inner, padded):
    chunks = [(inner, padded - inner)]
    at = 0
    while at < inner:
        width = WIDE if inner - at > WIDE else WIDE // 2
        chunks.append((at, width))
        at += width
    return chunks


def split_terms(value, terms):
    parts = []
    for _ in range(terms):
        part = value.astype(BF16)
        parts.append(part)
        value = value - part.astype(F32)
    return parts


def expand(value, first, width, terms=2):
    head = lax.broadcasted_iota(jnp.int32, (LANES, width), 0)
    lane = lax.broadcasted_iota(jnp.int32, (LANES, width), 1)
    one = jnp.where(head == first + lane // HEAD, 1.0, 0.0).astype(BF16)
    return dot(jnp.concatenate(split_terms(value, terms), 1), jnp.concatenate([one] * terms, 0))


def convolve(padded_ref, conv_ref, count):
    total = jnp.zeros((count, padded_ref.shape[1]), F32)
    for tap in range(4):
        total = total + padded_ref[pl.ds(RIM - 3 + tap, count), :] * conv_ref[tap : tap + 1, :]
    return total


def causal_mask():
    row = lax.broadcasted_iota(jnp.int32, (LANES, LANES), 0)
    col = lax.broadcasted_iota(jnp.int32, (LANES, LANES), 1)
    return (col <= row) & (row // Q == col // Q)


def prepare(level, padded_bc, steps, conv_bc, rate, query_ref, sums_ref, reach_ref, local):
    keys_t, cumul_s, cumul_t, scores_s, ends_s, steps_s, totals_s = local
    count = query_ref.shape[0]
    both = convolve(padded_bc, conv_bc, count)
    keys = both[:, :STATE].astype(BF16)
    query = both[:, STATE:].astype(BF16)
    query_ref[...] = query
    steps = jnp.maximum(steps, 0.0) + jnp.log1p(jnp.exp(-jnp.abs(steps)))
    steps_s[...] = steps
    decay = -steps * rate
    ones = jnp.where(causal_mask(), 1.0, 0.0).astype(BF16)
    before = jnp.zeros((1, LANES), F32)
    totals_s[...] = jnp.zeros_like(totals_s)
    for p in range(count // LANES):
        rows = slice(p * LANES, (p + 1) * LANES)
        terms = split_terms(decay[rows], 3)
        cumul = dot(ones, terms[2]) + dot(ones, terms[1]) + dot(ones, terms[0])
        cumul_s[rows, :] = cumul
        cumul_t[:, rows] = cumul.T
        keys_p = keys[rows].astype(F32).T.astype(BF16)
        keys_t[:, rows] = keys_p
        scores_s[rows, :] = dot(query[rows], keys_p) * level(0)
        for half in range(2):
            part = cumul[half * Q : (half + 1) * Q]
            total = part[Q - 1 : Q]
            at = slice(p * LANES + half * Q, p * LANES + (half + 1) * Q)
            ends_s[at, :] = jnp.exp(total - part)
            reach_ref[at, :] = jnp.exp(part + before)
            totals_s[2 * p + half : 2 * p + half + 1, :] = total
            before = before + total
    sums_ref[...] = jnp.broadcast_to(before, sums_ref.shape)


def mix_chunk(level, first, padded_s, conv_ref, skip, y_ref, query_ref, local):
    keys_t, cumul_s, cumul_t, scores_s, ends_s, steps_s, totals_s = local
    count, width = y_ref.shape
    stretches = count // Q
    pairs = count // LANES
    causal = causal_mask()
    convolved = convolve(padded_s, conv_ref, count)
    values = (convolved / (1.0 + jnp.exp(-convolved))).astype(BF16).astype(F32)
    driven = (values * expand(steps_s[...], first, width, 3)).astype(BF16)
    ended = (driven.astype(F32) * expand(ends_s[...], first, width)).astype(BF16)
    totals = expand(totals_s[...], first, width, 3)
    heads = width // HEAD
    turn = (LANES - first) % LANES
    left = lax.broadcasted_iota(jnp.int32, (LANES, LANES), 1) < HEAD
    upper = lax.broadcasted_iota(jnp.int32, (LANES, width), 0) < Q
    if not isinstance(first, int):
        first = pl.multiple_of(first, heads)
    states = []
    for p in range(pairs):
        rows = slice(p * LANES, (p + 1) * LANES)
        down = pltpu.roll(cumul_s[rows, :], turn, 1)
        along = cumul_t[pl.ds(first, heads), rows]
        scores = scores_s[rows, :]
        for two in range(heads // 2):
            cols = slice(two * LANES, (two + 1) * LANES)
            parts = []
            for h in (2 * two, 2 * two + 1):
                differ = down[:, h : h + 1] - along[h : h + 1, :]
                weight = jnp.exp(jnp.where(causal, differ, -1e30)) * scores
                parts.append(dot(weight.astype(BF16), driven[rows, cols]))
            y_ref[rows, cols] = (
                jnp.where(left, parts[0], parts[1]) + skip[:, cols] * values[rows, cols]
            )
        ended_p = ended[rows]
        keys_p = keys_t[:, rows]
        zero = jnp.zeros_like(ended_p)
        states.append(dot(keys_p, jnp.where(upper, ended_p, zero)))
        states.append(dot(keys_p, jnp.where(upper, zero, ended_p)))

    sums = [totals[i : i + 1] for i in range(stretches)]
    carried = [None] * stretches
    blocks, block_sums = states, sums
    for bit in range(stretches.bit_length() - 1):
        weight = level(bit + 1)
        for k in range(1, len(blocks), 2):
            passed = jnp.zeros((1, width), F32)
            for j in range(k << bit, (k + 1) << bit):
                term = blocks[k - 1] * (weight * jnp.exp(passed))
                carried[j] = term if carried[j] is None else carried[j] + term
                passed = passed + sums[j]
        merged = [
            blocks[k] * jnp.exp(block_sums[k + 1]) + blocks[k + 1] for k in range(0, len(blocks), 2)
        ]
        block_sums = [block_sums[k] + block_sums[k + 1] for k in range(0, len(blocks), 2)]
        blocks = merged
    grown = expand(jnp.exp(cumul_s[...]), first, width)
    for j in range(1, stretches):
        rows = slice(j * Q, (j + 1) * Q)
        y_ref[rows, :] += grown[rows] * dot(query_ref[rows, :], carried[j].astype(BF16))
    return blocks[0]


def finish_chunk(first, live_to, y, cross, reach_ref, query_ref, out_ref):
    count, width = out_ref.shape
    output = y + expand(reach_ref[...], first, width) * dot(query_ref[...], cross)
    squares = output * output
    row = lax.broadcasted_iota(jnp.int32, (LANES, LANES), 0)
    col = lax.broadcasted_iota(jnp.int32, (LANES, LANES), 1)
    same = jnp.where(row // HEAD == col // HEAD, 1.0 / HEAD, 0.0).astype(BF16)
    same = jnp.concatenate([same, same], 0)
    live = lax.broadcasted_iota(jnp.int32, (count, LANES), 0) < live_to
    for two in range(width // LANES):
        cols = slice(two * LANES, (two + 1) * LANES)
        mean = dot(jnp.concatenate(split_terms(squares[:, cols], 2), 1), same)
        out_ref[:, cols] = jnp.where(live, output[:, cols] * lax.rsqrt(mean + 1e-05), 0.0).astype(BF16)


def local_scratch(count):
    return [
        pltpu.VMEM((STATE, count), BF16),
        pltpu.VMEM((count, LANES), F32),
        pltpu.VMEM((LANES, count), F32),
        pltpu.VMEM((count, LANES), F32),
        pltpu.VMEM((count, LANES), F32),
        pltpu.VMEM((count, LANES), F32),
        pltpu.VMEM((max(8, count // Q), LANES), F32),
    ]


def mix_kernel(
    level_ref, raw_ref, bc_ref, step_ref, conv_ref, conv_bc_ref, rate_ref, skip_ref,
    y_ref, state_ref, sums_ref, reach_ref, query_ref, padded_s, padded_bc, *local,
):
    chunk = pl.program_id(0)
    level = lambda at: level_ref[0, at].astype(F32) / 256.0

    @pl.when(chunk == 0)
    def _():
        padded_bc[...] = bc_ref[...].astype(F32)
        steps = step_ref[pl.ds(RIM, y_ref.shape[0]), :]
        prepare(level, padded_bc, steps, conv_bc_ref, rate_ref[...], query_ref, sums_ref, reach_ref, local)

    padded_s[...] = raw_ref[...].astype(F32)
    first = chunk * (WIDE // HEAD)
    state = mix_chunk(level, first, padded_s, conv_ref, skip_ref[...], y_ref, query_ref, local)
    state_ref[...] = state.astype(BF16)


def mix(raw, steps, conv_w, rate, skip, level_w, count):
    inner = conv_w.shape[1] - 2 * STATE
    total = raw.shape[0]
    whole = lambda shape: pl.BlockSpec(shape, lambda i: (0, 0))
    part = lambda rows: pl.BlockSpec((rows, WIDE), lambda i: (0, i))
    tail = lambda rows: pl.BlockSpec((rows, 2 * STATE), lambda i: (0, inner // (2 * STATE)))
    return pl.pallas_call(
        mix_kernel,
        grid=(inner // WIDE,),
        in_specs=[
            pl.BlockSpec(memory_space=pltpu.SMEM),
            part(total),
            tail(total),
            whole((total, LANES)),
            part(4),
            tail(4),
            whole((1, LANES)),
            part(1),
        ],
        out_specs=(part(count), part(STATE), whole((8, LANES)), whole((count, LANES)), whole((count, STATE))),
        out_shape=(
            jax.ShapeDtypeStruct((count, inner), F32),
            jax.ShapeDtypeStruct((STATE, inner), BF16),
            jax.ShapeDtypeStruct((8, LANES), F32),
            jax.ShapeDtypeStruct((count, LANES), F32),
            jax.ShapeDtypeStruct((count, STATE), BF16),
        ),
        scratch_shapes=[
            pltpu.VMEM((total, WIDE), F32),
            pltpu.VMEM((total, 2 * STATE), F32),
        ]
        + local_scratch(count),
        compiler_params=pltpu.CompilerParams(vmem_limit_bytes=48 * 2**20),
        name="mix",
    )(level_w, raw, raw, steps, conv_w, conv_w, rate, skip)


def finish_kernel(live_ref, y_ref, cross_ref, reach_ref, query_ref, out_ref):
    first = pl.program_id(0) * (WIDE // HEAD)
    finish_chunk(first, live_ref[0], y_ref[...], cross_ref[...], reach_ref, query_ref, out_ref)


def finish(live, y, cross, reach, query):
    count, inner = y.shape
    whole = lambda shape: pl.BlockSpec(shape, lambda i: (0, 0))
    part = lambda rows: pl.BlockSpec((rows, WIDE), lambda i: (0, i))
    return pl.pallas_call(
        finish_kernel,
        grid=(inner // WIDE,),
        in_specs=[
            pl.BlockSpec(memory_space=pltpu.SMEM),
            part(count),
            part(STATE),
            whole((count, LANES)),
            whole((count, STATE)),
        ],
        out_specs=part(count),
        out_shape=jax.ShapeDtypeStruct((count, inner), BF16),
        compiler_params=pltpu.CompilerParams(vmem_limit_bytes=48 * 2**20),
        name="finish",
    )(live, y, cross, reach, query)


def swapped(value, axis, stride):
    mask = 2**stride
    pairs = [(source, source ^ mask) for source in range(lax.axis_size(axis))]
    return lax.ppermute(value, axis, pairs)


def fused_kernel(
    nz, n, inner, level_ref, live_ref, tok_ref, w_ref, conv_ref, rate_ref, skip_ref, out_ref,
    ext, wbuf, tok_sem, rim_sem, own_sem, send_sem, recv_sem, core_send, core_recv,
    y_s, out_s, padded_s, query_s, reach_s, sums_s, all_sums, own_state, pair_in, pair_state, quad_in,
    quad_state, third_in, cross_s, sum_send, sum_recv, state_send, state_recv, out_sem, *local,
):
    seq = lax.axis_index("seq")
    dp = lax.axis_index("dp")
    nseq = nz * n
    z, x = seq // n, seq % n
    y, core = dp // 2, dp % 2
    rows = w_ref.shape[0]
    count = tok_ref.shape[0]
    padded = w_ref.shape[1]
    chunks = chunk_list(inner, padded)
    after = (seq + 1) % nseq
    prior = (seq + nseq - 1) % nseq

    def place(dz, da, db):
        dx = da * (1 - core) + db * core
        dy = da * core + db * (1 - core)
        return ((z + dz) % nz) * n + (x + dx) % n, ((y + dy) % n) * 2 + core

    def rows_of(device):
        at = device[0] * (2 * n) + device[1]
        return pl.ds(pl.multiple_of(at * rows, rows), rows)

    offsets = [(dz, da, db) for dz in range(nz) for da in range(n) for db in range(n)]
    other = (seq, y * 2 + 1 - core)
    along_seq = [((seq + by) % nseq, dp) for by in range(1, nseq)]

    barrier = pltpu.get_barrier_semaphore()
    greeted = along_seq + [(seq, ((y + by) % n) * 2 + core) for by in range(1, n)] + [other]
    for device in greeted:
        pl.semaphore_signal(barrier, inc=1, device_id=device, device_id_type=MESH)
    pl.semaphore_wait(barrier, len(greeted))

    rim = pltpu.make_async_remote_copy(
        src_ref=tok_ref.at[pl.ds(count - RIM, RIM)],
        dst_ref=ext.at[pl.ds(0, RIM)],
        send_sem=rim_sem.at[0],
        recv_sem=rim_sem.at[1],
        device_id=(after, dp),
        device_id_type=MESH,
    )
    own_rows = rows_of((seq, dp))
    number = {offset: at for at, offset in enumerate(offsets)}
    sends = []

    def link_copy(c, offset, step):
        at, width = chunks[c]
        cols = pl.ds(at, width)
        where = rows_of(place(*offset))
        mine = offset == (0, 0, 0)
        lands = tuple((o - s) % m for o, s, m in zip(offset, step, (nz, n, n)))
        slot = number[lands]
        return pltpu.make_async_remote_copy(
            src_ref=w_ref.at[:, cols] if mine else wbuf.at[where, cols],
            dst_ref=wbuf.at[where, cols],
            send_sem=send_sem.at[c, slot],
            recv_sem=recv_sem.at[c, slot],
            device_id=place(*step),
            device_id_type=MESH,
        )

    def arrived(c, offset):
        at, width = chunks[c]
        ref = wbuf.at[rows_of(place(*offset)), pl.ds(at, width)]
        pltpu.make_async_copy(ref, ref, recv_sem.at[c, number[offset]]).wait()

    def core_copy(c, offset):
        at, width = chunks[c]
        cols = pl.ds(at, width)
        where = rows_of(place(*offset))
        mine = offset == (0, 0, 0)
        return pltpu.make_async_remote_copy(
            src_ref=w_ref.at[:, cols] if mine else wbuf.at[where, cols],
            dst_ref=wbuf.at[where, cols],
            send_sem=core_send.at[c, number[offset]],
            recv_sem=core_recv.at[c, number[offset]],
            device_id=other,
            device_id_type=MESH,
        )

    def core_arrived(c, offset):
        dz, da, db = offset
        at, width = chunks[c]
        theirs = 1 - core
        dx = da * (1 - theirs) + db * theirs
        dy = da * theirs + db * (1 - theirs)
        device = ((z + dz) % nz) * n + (x + dx) % n, ((y + dy) % n) * 2 + theirs
        ref = wbuf.at[rows_of(device), pl.ds(at, width)]
        pltpu.make_async_copy(ref, ref, core_recv.at[c, number[offset]]).wait()

    def start(copy):
        copy.start()
        sends.append(copy)

    def send_on(c, offset):
        if offset[1] == 0 and offset[2] == 0:
            for da in range(1, n):
                start(link_copy(c, offset, (0, da, 0)))
        if offset[2] == 0:
            for db in range(1, n):
                start(link_copy(c, offset, (0, 0, db)))
        start(core_copy(c, offset))

    def send_own(c):
        for dz in range(1, nz):
            start(link_copy(c, (0, 0, 0), (dz, 0, 0)))
        send_on(c, (0, 0, 0))

    def forward(c, stage):
        for offset in offsets[1:]:
            if (2 if offset[2] else 1 if offset[1] else 0) == stage:
                arrived(c, offset)
                send_on(c, offset)

    level = lambda at: level_ref[0, at].astype(F32) / 256.0
    bits = (count // Q).bit_length() - 1

    def sum_copy(by):
        return pltpu.make_async_remote_copy(
            src_ref=sums_s,
            dst_ref=all_sums.at[seq],
            send_sem=sum_send.at[by],
            recv_sem=sum_recv.at[by],
            device_id=((seq + by) % nseq, dp),
            device_id_type=MESH,
        )

    def multiply(c):
        for offset in offsets:
            core_arrived(c, offset)
        at, width = chunks[c]
        if c == 0:
            mid = at + 2 * STATE
            padded_s[:, 0 : 2 * STATE] = dot(ext[...], wbuf[:, at:mid]).astype(BF16).astype(F32)
            steps = dot(ext[...], wbuf[:, mid:])[RIM:]
            conv_bc = conv_ref.at[:, at:mid]
            prepare(
                level, padded_s.at[:, 0 : 2 * STATE], steps, conv_bc, rate_ref[...],
                query_s, sums_s, reach_s, local,
            )
            all_sums[seq] = sums_s[...]
            for by in range(1, nseq):
                sum_copy(by).start()
            return

        @pl.loop(0, width // 256)
        def _(tile):
            cols = pl.ds(pl.multiple_of(at + tile * 256, 256), 256)
            lands = pl.ds(pl.multiple_of(tile * 256, 256), 256)
            padded_s[:, lands] = dot(ext[...], wbuf[:, cols]).astype(BF16).astype(F32)

        cols = pl.ds(at, width)
        state = mix_chunk(
            level, at // HEAD, padded_s.at[:, 0:width], conv_ref.at[:, cols], skip_ref[:, cols],
            y_s.at[:, cols], query_s, local,
        )
        own_state[:, cols] = state.astype(BF16)
        state_copy(c, 0).start()

    def state_copy(c, hop):
        at, width = chunks[c]
        cols = pl.ds(at, width)
        source, target, device = (
            (own_state, pair_in, (seq + 1 - 2 * x, dp)),
            (pair_state, quad_in, ((seq + n) % nseq, dp)),
            (quad_state, quad_in, ((seq + n) % nseq, dp)),
            (quad_in, third_in, ((seq + n) % nseq, dp)),
        )[hop]
        return pltpu.make_async_remote_copy(
            src_ref=source.at[:, cols],
            dst_ref=target.at[:, cols],
            send_sem=state_send.at[c, hop],
            recv_sem=state_recv.at[c, hop],
            device_id=device,
            device_id_type=MESH,
        )

    def sums_of(c, device):
        at, width = chunks[c]
        return expand(all_sums[device], at // HEAD, width, 3)[0:1]

    upper = x.astype(F32)
    odd = z % 2

    def passed_pair(c):
        return upper * sums_of(c, z * n)

    def exchange(c, stage):
        at, width = chunks[c]
        cols = pl.ds(at, width)
        if stage == 0:
            state_copy(c, 0).wait_recv()
            mine = own_state[:, cols].astype(F32)
            theirs = pair_in[:, cols].astype(F32)
            cross_s[:, cols] = theirs * (upper * level(bits + 1))
            first = jnp.where(x == 0, mine, theirs)
            second = jnp.where(x == 0, theirs, mine)
            pair = first * jnp.exp(sums_of(c, z * n + 1)) + second
            pair_state[:, cols] = pair.astype(BF16)

            @pl.when(odd == 0)
            def _():
                state_copy(c, 1).start()

        elif stage == 1:

            @pl.when(odd == 1)
            def _():
                state_copy(c, 1).wait_recv()
                lower = quad_in[:, cols].astype(F32)
                cross_s[:, cols] += lower * (level(bits + 2) * jnp.exp(passed_pair(c)))
                pair_sum = sums_of(c, z * n) + sums_of(c, z * n + 1)
                quad = lower * jnp.exp(pair_sum) + pair_state[:, cols].astype(F32)
                quad_state[:, cols] = quad.astype(BF16)

            @pl.when(z == 1)
            def _():
                state_copy(c, 2).start()

        else:

            @pl.when(z == 2)
            def _():
                state_copy(c, 2).wait_recv()
                state_copy(c, 3).start()
                lower = quad_in[:, cols].astype(F32)
                cross_s[:, cols] += lower * (level(bits + 3) * jnp.exp(passed_pair(c)))

            @pl.when(z == 3)
            def _():
                state_copy(c, 3).wait_recv()
                lower = third_in[:, cols].astype(F32)
                before = passed_pair(c) + sums_of(c, z * n - 1) + sums_of(c, z * n - 2)
                cross_s[:, cols] += lower * (level(bits + 3) * jnp.exp(before))

            view = out_s.at[:, cols]
            finish_chunk(
                at // HEAD, live_ref[0], y_s[:, cols], cross_s[:, cols].astype(BF16), reach_s, query_s, view
            )
            out_copy(c).start()

    def out_copy(c):
        at, width = chunks[c]
        cols = pl.ds(at, width)
        return pltpu.make_async_copy(out_s.at[:, cols], out_ref.at[:, cols], out_sem.at[c])

    send_own(0)
    rim.start()
    tokens_in = pltpu.make_async_copy(tok_ref, ext.at[pl.ds(RIM, count)], tok_sem.at[0])
    tokens_in.start()
    own_in = pltpu.make_async_copy(w_ref, wbuf.at[own_rows], own_sem.at[0])
    own_in.start()
    send_own(1)
    rim.wait()
    tokens_in.wait()
    own_in.wait()

    @pl.when(seq == 0)
    def _():
        ext[0:RIM, :] = jnp.zeros((RIM, ext.shape[1]), BF16)

    last = len(chunks) - 1
    for step in range(last + 7):
        if step <= last:
            forward(step, 0)
        if step + 2 <= last:
            send_own(step + 2)
        if 0 <= step - 1 <= last:
            forward(step - 1, 1)
        if 0 <= step - 2 <= last:
            forward(step - 2, 2)
        for stage in (2, 1, 0):
            if 1 <= step - 4 - stage <= last:
                if step - 4 - stage == 1 and stage == 0:
                    for by in range(1, nseq):
                        sum_copy(by).wait_recv()
                exchange(step - 4 - stage, stage)
        if 0 <= step - 3 <= last:
            multiply(step - 3)
    for copy in sends:
        copy.wait_send()
    for by in range(1, nseq):
        sum_copy(by).wait_send()
    for c in range(1, last + 1):
        out_copy(c).wait()
        state_copy(c, 0).wait_send()

        @pl.when(odd == 0)
        def _():
            state_copy(c, 1).wait_send()

        @pl.when(z == 1)
        def _():
            state_copy(c, 2).wait_send()

        @pl.when(z == 2)
        def _():
            state_copy(c, 3).wait_send()


def fused(tokens, w_in, conv_w, rate, skip, level_w, live, nseq, ndp):
    count, depth = tokens.shape
    padded = -(-w_in.shape[1] // LANES) * LANES
    w_in = jnp.pad(w_in, ((0, 0), (0, padded - w_in.shape[1])))
    inner = conv_w.shape[1] - 2 * STATE
    n = ndp // 2
    nz = nseq // n
    total = count + RIM
    shards = nz * n * n
    chunks = len(chunk_list(inner, padded))
    smem = pl.BlockSpec(memory_space=pltpu.SMEM)
    vmem = pl.BlockSpec(memory_space=pltpu.VMEM)
    anywhere = pl.BlockSpec(memory_space=pl.ANY)
    state = pltpu.VMEM((STATE, inner), BF16)
    return pl.pallas_call(
        functools.partial(fused_kernel, nz, n, inner),
        out_shape=jax.ShapeDtypeStruct((count, inner), BF16),
        in_specs=[smem, smem, anywhere, anywhere, vmem, vmem, vmem],
        out_specs=anywhere,
        scratch_shapes=[
            pltpu.VMEM((total, depth), BF16),
            pltpu.VMEM((depth, padded), BF16),
            pltpu.SemaphoreType.DMA((1,)),
            pltpu.SemaphoreType.DMA((2,)),
            pltpu.SemaphoreType.DMA((1,)),
        ]
        + [pltpu.SemaphoreType.DMA((chunks, shards))] * 4
        + [
            pltpu.VMEM((count, inner), F32),
            pltpu.VMEM((count, inner), BF16),
            pltpu.VMEM((total, WIDE), F32),
            pltpu.VMEM((count, STATE), BF16),
            pltpu.VMEM((count, LANES), F32),
            pltpu.VMEM((8, LANES), F32),
            pltpu.VMEM((nseq, 8, LANES), F32),
        ]
        + [state] * 6
        + [
            pltpu.VMEM((STATE, inner), F32),
            pltpu.SemaphoreType.DMA((nseq,)),
            pltpu.SemaphoreType.DMA((nseq,)),
            pltpu.SemaphoreType.DMA((chunks, 4)),
            pltpu.SemaphoreType.DMA((chunks, 4)),
            pltpu.SemaphoreType.DMA((chunks,)),
        ]
        + local_scratch(count),
        compiler_params=pltpu.CompilerParams(
            collective_id=0, has_side_effects=True, vmem_limit_bytes=60 * 2**20
        ),
        name="fused",
    )(level_w, live, tokens, w_in, conv_w, rate, skip)


def body(tokens, w_in, conv_w, a_rate, d_skip, level_w, lengths):
    token_rows = tokens.reshape(-1, tokens.shape[-1])
    count = token_rows.shape[0]
    heads = a_rate.shape[0]
    inner = conv_w.shape[1] - 2 * STATE
    nseq = lax.axis_size("seq")
    rate = jnp.pad(a_rate[None, :], ((0, 0), (0, LANES - heads)))
    skip = jnp.repeat(d_skip, HEAD)[None, :]
    live = lengths - lax.axis_index("seq") * count
    ndp = lax.axis_size("dp")
    if (nseq, ndp) == (8, 4):
        out = fused(token_rows, w_in, conv_w, rate, skip, level_w, live, nseq, ndp)
        return out.reshape(1, count, inner)
    channels = conv_w.shape[1]
    edge = lax.ppermute(token_rows[count - RIM :], "seq", [(i, i + 1) for i in range(nseq - 1)])
    full = lax.all_gather(w_in, ("seq", "dp"), axis=0, tiled=True)
    projected = dot(jnp.concatenate([edge, token_rows], 0), full)
    raw = projected[:, :channels].astype(BF16)
    steps = jnp.pad(projected[:, channels:], ((0, 0), (0, LANES - heads)))
    y, block_state, sums, reach, query = mix(raw, steps, conv_w, rate, skip, level_w, count)
    level_wt = level_w.reshape(-1).astype(F32) / 256.0
    position = lax.axis_index("seq")
    wide = lambda value: jnp.repeat(value, HEAD)[None, :]
    block_state = block_state.astype(F32)
    block_total = sums[0, :heads]
    cross_state = jnp.zeros_like(block_state)
    passed = jnp.zeros_like(block_total)
    local_bits = (count // Q).bit_length() - 1
    for level in range(nseq.bit_length() - 1):
        other_state = swapped(block_state.astype(BF16), "seq", level).astype(F32)
        other_total = swapped(block_total, "seq", level)
        upper = (jnp.right_shift(position, level) & 1).astype(F32)
        weight = upper * level_wt[local_bits + level + 1]
        cross_state = cross_state + weight * wide(jnp.exp(passed)) * other_state
        passed = passed + upper * other_total
        block_state = jnp.where(
            upper > 0.5,
            other_state * wide(jnp.exp(block_total)) + block_state,
            block_state * wide(jnp.exp(other_total)) + other_state,
        )
        block_total = block_total + other_total
    out = finish(live, y, cross_state.astype(BF16), reach, query)
    return out.reshape(1, count, inner)


def solution(mesh):
    in_specs = (P("dp", "seq", None), P(("seq", "dp"), None), P(), P(), P(), P("dp", None), P("dp"))
    out_specs = P("dp", "seq", None)
    return jax.shard_map(body, mesh=mesh, in_specs=in_specs, out_specs=out_specs, check_vma=False)
```

```python
import functools

import jax
import jax.numpy as jnp
from jax import lax
from jax.experimental import pallas as pl
from jax.experimental.pallas import tpu as pltpu
from jax.sharding import PartitionSpec as P

STATE = 128
Q = 64
RIM = 16
LANES = 128
WIDE = 512
TURNED = 3
HEAD = 64
MESH = pl.DeviceIdType.MESH
F32 = jnp.float32
BF16 = jnp.bfloat16


def dot(a, b):
    return jnp.dot(a, b, preferred_element_type=F32)


def chunk_list(inner, padded):
    chunks = [(inner, padded - inner)]
    at = 0
    while at < inner:
        width = WIDE // 2 if inner - at <= WIDE // 2 or len(chunks) == TURNED else WIDE
        chunks.append((at, width))
        at += width
    return chunks


def split_terms(value, terms):
    parts = []
    for _ in range(terms):
        part = value.astype(BF16)
        parts.append(part)
        value = value - part.astype(F32)
    return parts


def expand(value, first, width, terms=2):
    head = lax.broadcasted_iota(jnp.int32, (LANES, width), 0)
    lane = lax.broadcasted_iota(jnp.int32, (LANES, width), 1)
    one = jnp.where(head == first + lane // HEAD, 1.0, 0.0).astype(BF16)
    return dot(jnp.concatenate(split_terms(value, terms), 1), jnp.concatenate([one] * terms, 0))


def convolve(padded_ref, conv_ref, count):
    total = jnp.zeros((count, padded_ref.shape[1]), F32)
    for tap in range(4):
        total = total + padded_ref[pl.ds(RIM - 3 + tap, count), :] * conv_ref[tap : tap + 1, :]
    return total


def causal_mask():
    row = lax.broadcasted_iota(jnp.int32, (LANES, LANES), 0)
    col = lax.broadcasted_iota(jnp.int32, (LANES, LANES), 1)
    return (col <= row) & (row // Q == col // Q)


def prepare(level, padded_bc, steps, conv_bc, rate, query_ref, sums_ref, reach_ref, local):
    keys_t, cumul_s, cumul_t, scores_s, ends_s, steps_s, totals_s = local
    count = query_ref.shape[0]
    both = convolve(padded_bc, conv_bc, count)
    keys = both[:, :STATE].astype(BF16)
    query = both[:, STATE:].astype(BF16)
    query_ref[...] = query
    steps = jnp.maximum(steps, 0.0) + jnp.log1p(jnp.exp(-jnp.abs(steps)))
    steps_s[...] = steps
    decay = -steps * rate
    ones = jnp.where(causal_mask(), 1.0, 0.0).astype(BF16)
    before = jnp.zeros((1, LANES), F32)
    totals_s[...] = jnp.zeros_like(totals_s)
    for p in range(count // LANES):
        rows = slice(p * LANES, (p + 1) * LANES)
        terms = split_terms(decay[rows], 3)
        cumul = dot(ones, terms[2]) + dot(ones, terms[1]) + dot(ones, terms[0])
        cumul_s[rows, :] = cumul
        cumul_t[:, rows] = cumul.T
        keys_p = keys[rows].astype(F32).T.astype(BF16)
        keys_t[:, rows] = keys_p
        scores_s[rows, :] = dot(query[rows], keys_p) * level(0)
        for half in range(2):
            part = cumul[half * Q : (half + 1) * Q]
            total = part[Q - 1 : Q]
            at = slice(p * LANES + half * Q, p * LANES + (half + 1) * Q)
            ends_s[at, :] = jnp.exp(total - part)
            reach_ref[at, :] = jnp.exp(part + before)
            totals_s[2 * p + half : 2 * p + half + 1, :] = total
            before = before + total
    sums_ref[...] = jnp.broadcast_to(before, sums_ref.shape)


def mix_chunk(level, first, padded_s, conv_ref, skip, y_ref, query_ref, local):
    keys_t, cumul_s, cumul_t, scores_s, ends_s, steps_s, totals_s = local
    count, width = y_ref.shape
    stretches = count // Q
    pairs = count // LANES
    causal = causal_mask()
    convolved = convolve(padded_s, conv_ref, count)
    values = (convolved / (1.0 + jnp.exp(-convolved))).astype(BF16).astype(F32)
    driven = (values * expand(steps_s[...], first, width, 3)).astype(BF16)
    ended = (driven.astype(F32) * expand(ends_s[...], first, width)).astype(BF16)
    totals = expand(totals_s[...], first, width, 3)
    heads = width // HEAD
    turn = (LANES - first) % LANES
    left = lax.broadcasted_iota(jnp.int32, (LANES, LANES), 1) < HEAD
    upper = lax.broadcasted_iota(jnp.int32, (LANES, width), 0) < Q
    if not isinstance(first, int):
        first = pl.multiple_of(first, heads)
    states = []
    for p in range(pairs):
        rows = slice(p * LANES, (p + 1) * LANES)
        down = pltpu.roll(cumul_s[rows, :], turn, 1)
        along = cumul_t[pl.ds(first, heads), rows]
        scores = scores_s[rows, :]
        for two in range(heads // 2):
            cols = slice(two * LANES, (two + 1) * LANES)
            parts = []
            for h in (2 * two, 2 * two + 1):
                differ = down[:, h : h + 1] - along[h : h + 1, :]
                weight = jnp.exp(jnp.where(causal, differ, -1e30)) * scores
                parts.append(dot(weight.astype(BF16), driven[rows, cols]))
            y_ref[rows, cols] = (
                jnp.where(left, parts[0], parts[1]) + skip[:, cols] * values[rows, cols]
            )
        ended_p = ended[rows]
        keys_p = keys_t[:, rows]
        zero = jnp.zeros_like(ended_p)
        states.append(dot(keys_p, jnp.where(upper, ended_p, zero)))
        states.append(dot(keys_p, jnp.where(upper, zero, ended_p)))

    sums = [totals[i : i + 1] for i in range(stretches)]
    carried = [None] * stretches
    blocks, block_sums = states, sums
    for bit in range(stretches.bit_length() - 1):
        weight = level(bit + 1)
        for k in range(1, len(blocks), 2):
            passed = jnp.zeros((1, width), F32)
            for j in range(k << bit, (k + 1) << bit):
                term = blocks[k - 1] * (weight * jnp.exp(passed))
                carried[j] = term if carried[j] is None else carried[j] + term
                passed = passed + sums[j]
        merged = [
            blocks[k] * jnp.exp(block_sums[k + 1]) + blocks[k + 1] for k in range(0, len(blocks), 2)
        ]
        block_sums = [block_sums[k] + block_sums[k + 1] for k in range(0, len(blocks), 2)]
        blocks = merged
    grown = expand(jnp.exp(cumul_s[...]), first, width)
    for j in range(1, stretches):
        rows = slice(j * Q, (j + 1) * Q)
        y_ref[rows, :] += grown[rows] * dot(query_ref[rows, :], carried[j].astype(BF16))
    return blocks[0]


def finish_chunk(first, live_to, y, cross, reach_ref, query_ref, out_ref):
    count, width = out_ref.shape
    output = y + expand(reach_ref[...], first, width) * dot(query_ref[...], cross)
    squares = output * output
    row = lax.broadcasted_iota(jnp.int32, (LANES, LANES), 0)
    col = lax.broadcasted_iota(jnp.int32, (LANES, LANES), 1)
    same = jnp.where(row // HEAD == col // HEAD, 1.0 / HEAD, 0.0).astype(BF16)
    same = jnp.concatenate([same, same], 0)
    live = lax.broadcasted_iota(jnp.int32, (count, LANES), 0) < live_to
    for two in range(width // LANES):
        cols = slice(two * LANES, (two + 1) * LANES)
        mean = dot(jnp.concatenate(split_terms(squares[:, cols], 2), 1), same)
        out_ref[:, cols] = jnp.where(live, output[:, cols] * lax.rsqrt(mean + 1e-05), 0.0).astype(BF16)


def local_scratch(count):
    return [
        pltpu.VMEM((STATE, count), BF16),
        pltpu.VMEM((count, LANES), F32),
        pltpu.VMEM((LANES, count), F32),
        pltpu.VMEM((count, LANES), F32),
        pltpu.VMEM((count, LANES), F32),
        pltpu.VMEM((count, LANES), F32),
        pltpu.VMEM((max(8, count // Q), LANES), F32),
    ]


def mix_kernel(
    level_ref, raw_ref, bc_ref, step_ref, conv_ref, conv_bc_ref, rate_ref, skip_ref,
    y_ref, state_ref, sums_ref, reach_ref, query_ref, padded_s, padded_bc, *local,
):
    chunk = pl.program_id(0)
    level = lambda at: level_ref[0, at].astype(F32) / 256.0

    @pl.when(chunk == 0)
    def _():
        padded_bc[...] = bc_ref[...].astype(F32)
        steps = step_ref[pl.ds(RIM, y_ref.shape[0]), :]
        prepare(level, padded_bc, steps, conv_bc_ref, rate_ref[...], query_ref, sums_ref, reach_ref, local)

    padded_s[...] = raw_ref[...].astype(F32)
    first = chunk * (WIDE // HEAD)
    state = mix_chunk(level, first, padded_s, conv_ref, skip_ref[...], y_ref, query_ref, local)
    state_ref[...] = state.astype(BF16)


def mix(raw, steps, conv_w, rate, skip, level_w, count):
    inner = conv_w.shape[1] - 2 * STATE
    total = raw.shape[0]
    whole = lambda shape: pl.BlockSpec(shape, lambda i: (0, 0))
    part = lambda rows: pl.BlockSpec((rows, WIDE), lambda i: (0, i))
    tail = lambda rows: pl.BlockSpec((rows, 2 * STATE), lambda i: (0, inner // (2 * STATE)))
    return pl.pallas_call(
        mix_kernel,
        grid=(inner // WIDE,),
        in_specs=[
            pl.BlockSpec(memory_space=pltpu.SMEM),
            part(total),
            tail(total),
            whole((total, LANES)),
            part(4),
            tail(4),
            whole((1, LANES)),
            part(1),
        ],
        out_specs=(part(count), part(STATE), whole((8, LANES)), whole((count, LANES)), whole((count, STATE))),
        out_shape=(
            jax.ShapeDtypeStruct((count, inner), F32),
            jax.ShapeDtypeStruct((STATE, inner), BF16),
            jax.ShapeDtypeStruct((8, LANES), F32),
            jax.ShapeDtypeStruct((count, LANES), F32),
            jax.ShapeDtypeStruct((count, STATE), BF16),
        ),
        scratch_shapes=[
            pltpu.VMEM((total, WIDE), F32),
            pltpu.VMEM((total, 2 * STATE), F32),
        ]
        + local_scratch(count),
        compiler_params=pltpu.CompilerParams(vmem_limit_bytes=48 * 2**20),
        name="mix",
    )(level_w, raw, raw, steps, conv_w, conv_w, rate, skip)


def finish_kernel(live_ref, y_ref, cross_ref, reach_ref, query_ref, out_ref):
    first = pl.program_id(0) * (WIDE // HEAD)
    finish_chunk(first, live_ref[0], y_ref[...], cross_ref[...], reach_ref, query_ref, out_ref)


def finish(live, y, cross, reach, query):
    count, inner = y.shape
    whole = lambda shape: pl.BlockSpec(shape, lambda i: (0, 0))
    part = lambda rows: pl.BlockSpec((rows, WIDE), lambda i: (0, i))
    return pl.pallas_call(
        finish_kernel,
        grid=(inner // WIDE,),
        in_specs=[
            pl.BlockSpec(memory_space=pltpu.SMEM),
            part(count),
            part(STATE),
            whole((count, LANES)),
            whole((count, STATE)),
        ],
        out_specs=part(count),
        out_shape=jax.ShapeDtypeStruct((count, inner), BF16),
        compiler_params=pltpu.CompilerParams(vmem_limit_bytes=48 * 2**20),
        name="finish",
    )(live, y, cross, reach, query)


def swapped(value, axis, stride):
    mask = 2**stride
    pairs = [(source, source ^ mask) for source in range(lax.axis_size(axis))]
    return lax.ppermute(value, axis, pairs)


def fused_kernel(
    nz, n, inner, level_ref, live_ref, tok_ref, w_ref, conv_ref, rate_ref, skip_ref, out_ref,
    ext, wbuf, tok_sem, rim_sem, own_sem, send_sem, recv_sem, core_send, core_recv,
    y_s, out_s, padded_s, query_s, reach_s, sums_s, all_sums, own_state, pair_in, pair_state, quad_in,
    quad_state, third_in, cross_s, sum_send, sum_recv, state_send, state_recv, out_sem, rates_s, *local,
):
    seq = lax.axis_index("seq")
    dp = lax.axis_index("dp")
    nseq = nz * n
    z, x = seq // n, seq % n
    y, core = dp // 2, dp % 2
    rows = w_ref.shape[0]
    count = tok_ref.shape[0]
    padded = w_ref.shape[1]
    chunks = chunk_list(inner, padded)
    after = (seq + 1) % nseq
    prior = (seq + nseq - 1) % nseq

    def place(dz, da, db):
        dx = da * (1 - core) + db * core
        dy = da * core + db * (1 - core)
        return ((z + dz) % nz) * n + (x + dx) % n, ((y + dy) % n) * 2 + core

    def rows_of(device):
        at = device[0] * (2 * n) + device[1]
        return pl.ds(pl.multiple_of(at * rows, rows), rows)

    offsets = [(dz, da, db) for dz in range(nz) for da in range(n) for db in range(n)]
    other = (seq, y * 2 + 1 - core)
    along_seq = [((seq + by) % nseq, dp) for by in range(1, nseq)]

    barrier = pltpu.get_barrier_semaphore()
    greeted = along_seq + [(seq, ((y + by) % n) * 2 + core) for by in range(1, n)] + [other]
    for device in greeted:
        pl.semaphore_signal(barrier, inc=1, device_id=device, device_id_type=MESH)
    pl.semaphore_wait(barrier, len(greeted))

    rim = pltpu.make_async_remote_copy(
        src_ref=tok_ref.at[pl.ds(count - RIM, RIM)],
        dst_ref=ext.at[pl.ds(0, RIM)],
        send_sem=rim_sem.at[0],
        recv_sem=rim_sem.at[1],
        device_id=(after, dp),
        device_id_type=MESH,
    )
    own_rows = rows_of((seq, dp))
    number = {offset: at for at, offset in enumerate(offsets)}
    sends = []

    def link_copy(c, offset, step):
        at, width = chunks[c]
        cols = pl.ds(at, width)
        where = rows_of(place(*offset))
        mine = offset == (0, 0, 0)
        lands = tuple((o - s) % m for o, s, m in zip(offset, step, (nz, n, n)))
        slot = number[lands]
        return pltpu.make_async_remote_copy(
            src_ref=w_ref.at[:, cols] if mine else wbuf.at[where, cols],
            dst_ref=wbuf.at[where, cols],
            send_sem=send_sem.at[c, slot],
            recv_sem=recv_sem.at[c, slot],
            device_id=place(*step),
            device_id_type=MESH,
        )

    def arrived(c, offset):
        at, width = chunks[c]
        ref = wbuf.at[rows_of(place(*offset)), pl.ds(at, width)]
        pltpu.make_async_copy(ref, ref, recv_sem.at[c, number[offset]]).wait()

    def core_copy(c, offset):
        at, width = chunks[c]
        cols = pl.ds(at, width)
        where = rows_of(place(*offset))
        mine = offset == (0, 0, 0)
        return pltpu.make_async_remote_copy(
            src_ref=w_ref.at[:, cols] if mine else wbuf.at[where, cols],
            dst_ref=wbuf.at[where, cols],
            send_sem=core_send.at[c, number[offset]],
            recv_sem=core_recv.at[c, number[offset]],
            device_id=other,
            device_id_type=MESH,
        )

    def core_arrived(c, offset):
        dz, da, db = offset
        at, width = chunks[c]
        theirs = 1 - core
        dx = da * (1 - theirs) + db * theirs
        dy = da * theirs + db * (1 - theirs)
        device = ((z + dz) % nz) * n + (x + dx) % n, ((y + dy) % n) * 2 + theirs
        ref = wbuf.at[rows_of(device), pl.ds(at, width)]
        pltpu.make_async_copy(ref, ref, core_recv.at[c, number[offset]]).wait()

    def start(copy):
        copy.start()
        sends.append(copy)

    sizes = (nz, n, n)

    def order_of(c):
        return (1, 2, 0) if c == TURNED else (0, 1, 2)

    def stage_of(c, offset):
        return max([at for at, axis in enumerate(order_of(c)) if offset[axis]], default=-1)

    def send_on(c, offset):
        for axis in order_of(c)[stage_of(c, offset) + 1 :]:
            for by in range(1, sizes[axis]):
                start(link_copy(c, offset, tuple(by if axis == at else 0 for at in range(3))))
        start(core_copy(c, offset))

    def send_own(c):
        send_on(c, (0, 0, 0))

    def forward(c, stage):
        for offset in offsets[1:]:
            if stage_of(c, offset) == stage:
                arrived(c, offset)
                send_on(c, offset)

    level = lambda at: level_ref[0, at].astype(F32) / 256.0
    bits = (count // Q).bit_length() - 1

    def sum_copy(by):
        return pltpu.make_async_remote_copy(
            src_ref=sums_s,
            dst_ref=all_sums.at[seq],
            send_sem=sum_send.at[by],
            recv_sem=sum_recv.at[by],
            device_id=((seq + by) % nseq, dp),
            device_id_type=MESH,
        )

    def multiply(c):
        for offset in offsets:
            core_arrived(c, offset)
        at, width = chunks[c]
        if c == 0:
            mid = at + 2 * STATE
            padded_s[:, 0 : 2 * STATE] = dot(ext[...], wbuf[:, at:mid]).astype(BF16).astype(F32)
            steps = dot(ext[...], wbuf[:, mid:])[RIM:]
            conv_bc = conv_ref.at[:, at:mid]
            prepare(
                level, padded_s.at[:, 0 : 2 * STATE], steps, conv_bc, rates_s[0:1],
                query_s, sums_s, reach_s, local,
            )
            all_sums[seq] = sums_s[...]
            for by in range(1, nseq):
                sum_copy(by).start()
            return

        @pl.loop(0, width // 256)
        def _(tile):
            cols = pl.ds(pl.multiple_of(at + tile * 256, 256), 256)
            lands = pl.ds(pl.multiple_of(tile * 256, 256), 256)
            padded_s[:, lands] = dot(ext[...], wbuf[:, cols]).astype(BF16).astype(F32)

        cols = pl.ds(at, width)
        state = mix_chunk(
            level, at // HEAD, padded_s.at[:, 0:width], conv_ref.at[:, cols], expand(rates_s[1:2], at // HEAD, width, 3),
            y_s.at[:, cols], query_s, local,
        )
        own_state[:, cols] = state.astype(BF16)
        state_copy(c, 0).start()

    def state_copy(c, hop):
        at, width = chunks[c]
        cols = pl.ds(at, width)
        source, target, device = (
            (own_state, pair_in, (seq + 1 - 2 * x, dp)),
            (pair_state, quad_in, ((seq + n) % nseq, dp)),
            (quad_state, quad_in, ((seq + n) % nseq, dp)),
            (quad_in, third_in, ((seq + n) % nseq, dp)),
        )[hop]
        return pltpu.make_async_remote_copy(
            src_ref=source.at[:, cols],
            dst_ref=target.at[:, cols],
            send_sem=state_send.at[c, hop],
            recv_sem=state_recv.at[c, hop],
            device_id=device,
            device_id_type=MESH,
        )

    def sums_of(c, device):
        at, width = chunks[c]
        return expand(all_sums[device], at // HEAD, width, 3)[0:1]

    upper = x.astype(F32)
    odd = z % 2

    def passed_pair(c):
        return upper * sums_of(c, z * n)

    def exchange(c, stage):
        at, width = chunks[c]
        cols = pl.ds(at, width)
        if stage == 0:
            state_copy(c, 0).wait_recv()
            mine = own_state[:, cols].astype(F32)
            theirs = pair_in[:, cols].astype(F32)
            cross_s[:, cols] = theirs * (upper * level(bits + 1))
            first = jnp.where(x == 0, mine, theirs)
            second = jnp.where(x == 0, theirs, mine)
            pair = first * jnp.exp(sums_of(c, z * n + 1)) + second
            pair_state[:, cols] = pair.astype(BF16)

            @pl.when(odd == 0)
            def _():
                state_copy(c, 1).start()

        elif stage == 1:

            @pl.when(odd == 1)
            def _():
                state_copy(c, 1).wait_recv()
                lower = quad_in[:, cols].astype(F32)
                cross_s[:, cols] += lower * (level(bits + 2) * jnp.exp(passed_pair(c)))
                pair_sum = sums_of(c, z * n) + sums_of(c, z * n + 1)
                quad = lower * jnp.exp(pair_sum) + pair_state[:, cols].astype(F32)
                quad_state[:, cols] = quad.astype(BF16)

            @pl.when(z == 1)
            def _():
                state_copy(c, 2).start()

        else:

            @pl.when(z == 2)
            def _():
                state_copy(c, 2).wait_recv()
                state_copy(c, 3).start()
                lower = quad_in[:, cols].astype(F32)
                cross_s[:, cols] += lower * (level(bits + 3) * jnp.exp(passed_pair(c)))

            @pl.when(z == 3)
            def _():
                state_copy(c, 3).wait_recv()
                lower = third_in[:, cols].astype(F32)
                before = passed_pair(c) + sums_of(c, z * n - 1) + sums_of(c, z * n - 2)
                cross_s[:, cols] += lower * (level(bits + 3) * jnp.exp(before))

            view = out_s.at[:, cols]
            finish_chunk(
                at // HEAD, live_ref[0], y_s[:, cols], cross_s[:, cols].astype(BF16), reach_s, query_s, view
            )
            out_copy(c).start()

    def out_copy(c):
        at, width = chunks[c]
        cols = pl.ds(at, width)
        return pltpu.make_async_copy(out_s.at[:, cols], out_ref.at[:, cols], out_sem.at[c])

    send_own(0)
    rim.start()
    tokens_in = pltpu.make_async_copy(tok_ref, ext.at[pl.ds(RIM, count)], tok_sem.at[0])
    tokens_in.start()
    own_in = pltpu.make_async_copy(w_ref, wbuf.at[own_rows], own_sem.at[0])
    own_in.start()
    send_own(1)
    send_own(2)
    rates_s[...] = jnp.zeros_like(rates_s)
    rates_s[0:1, 0 : rate_ref.shape[1]] = rate_ref[...]
    rates_s[1:2, 0 : rate_ref.shape[1]] = skip_ref[...]

    last = len(chunks) - 1
    for step in range(last + 7):
        if step <= last:
            forward(step, 0)
        if step + 3 <= last:
            send_own(step + 3)
        if 0 <= step - 1 <= last:
            forward(step - 1, 1)
        if step == 3:
            rim.wait()
            tokens_in.wait()
            own_in.wait()

            @pl.when(seq == 0)
            def _():
                ext[0:RIM, :] = jnp.zeros((RIM, ext.shape[1]), BF16)

        if 0 <= step - 3 <= last:
            multiply(step - 3)
        for stage in (0, 1, 2):
            if 1 <= step - 4 - stage <= last:
                if step - 4 - stage == 1 and stage == 0:
                    for by in range(1, nseq):
                        sum_copy(by).wait_recv()
                exchange(step - 4 - stage, stage)
        if 0 <= step - 2 <= last:
            forward(step - 2, 2)
    for copy in sends:
        copy.wait_send()
    for by in range(1, nseq):
        sum_copy(by).wait_send()
    for c in range(1, last + 1):
        out_copy(c).wait()
        state_copy(c, 0).wait_send()

        @pl.when(odd == 0)
        def _():
            state_copy(c, 1).wait_send()

        @pl.when(z == 1)
        def _():
            state_copy(c, 2).wait_send()

        @pl.when(z == 2)
        def _():
            state_copy(c, 3).wait_send()


def fused(tokens, w_in, conv_w, rate, skip, level_w, live, nseq, ndp):
    count, depth = tokens.shape
    padded = -(-w_in.shape[1] // LANES) * LANES
    w_in = jnp.pad(w_in, ((0, 0), (0, padded - w_in.shape[1])))
    inner = conv_w.shape[1] - 2 * STATE
    n = ndp // 2
    nz = nseq // n
    total = count + RIM
    shards = nz * n * n
    chunks = len(chunk_list(inner, padded))
    smem = pl.BlockSpec(memory_space=pltpu.SMEM)
    vmem = pl.BlockSpec(memory_space=pltpu.VMEM)
    anywhere = pl.BlockSpec(memory_space=pl.ANY)
    state = pltpu.VMEM((STATE, inner), BF16)
    return pl.pallas_call(
        functools.partial(fused_kernel, nz, n, inner),
        out_shape=jax.ShapeDtypeStruct((count, inner), BF16),
        in_specs=[smem, smem, anywhere, anywhere, vmem, vmem, vmem],
        out_specs=anywhere,
        scratch_shapes=[
            pltpu.VMEM((total, depth), BF16),
            pltpu.VMEM((depth, padded), BF16),
            pltpu.SemaphoreType.DMA((1,)),
            pltpu.SemaphoreType.DMA((2,)),
            pltpu.SemaphoreType.DMA((1,)),
        ]
        + [pltpu.SemaphoreType.DMA((chunks, shards))] * 4
        + [
            pltpu.VMEM((count, inner), F32),
            pltpu.VMEM((count, inner), BF16),
            pltpu.VMEM((total, WIDE), F32),
            pltpu.VMEM((count, STATE), BF16),
            pltpu.VMEM((count, LANES), F32),
            pltpu.VMEM((8, LANES), F32),
            pltpu.VMEM((nseq, 8, LANES), F32),
        ]
        + [state] * 6
        + [
            pltpu.VMEM((STATE, inner), F32),
            pltpu.SemaphoreType.DMA((nseq,)),
            pltpu.SemaphoreType.DMA((nseq,)),
            pltpu.SemaphoreType.DMA((chunks, 4)),
            pltpu.SemaphoreType.DMA((chunks, 4)),
            pltpu.SemaphoreType.DMA((chunks,)),
            pltpu.VMEM((8, LANES), F32),
        ]
        + local_scratch(count),
        compiler_params=pltpu.CompilerParams(
            collective_id=0, has_side_effects=True, vmem_limit_bytes=60 * 2**20
        ),
        name="fused",
    )(level_w, live, tokens, w_in, conv_w, rate, skip)


def body(tokens, w_in, conv_w, a_rate, d_skip, level_w, lengths):
    token_rows = tokens.reshape(-1, tokens.shape[-1])
    count = token_rows.shape[0]
    heads = a_rate.shape[0]
    inner = conv_w.shape[1] - 2 * STATE
    nseq = lax.axis_size("seq")
    live = lengths - lax.axis_index("seq") * count
    ndp = lax.axis_size("dp")
    if (nseq, ndp) == (8, 4):
        out = fused(token_rows, w_in, conv_w, a_rate[None, :], d_skip[None, :], level_w, live, nseq, ndp)
        return out.reshape(1, count, inner)
    rate = jnp.pad(a_rate[None, :], ((0, 0), (0, LANES - heads)))
    skip = jnp.repeat(d_skip, HEAD)[None, :]
    channels = conv_w.shape[1]
    edge = lax.ppermute(token_rows[count - RIM :], "seq", [(i, i + 1) for i in range(nseq - 1)])
    full = lax.all_gather(w_in, ("seq", "dp"), axis=0, tiled=True)
    projected = dot(jnp.concatenate([edge, token_rows], 0), full)
    raw = projected[:, :channels].astype(BF16)
    steps = jnp.pad(projected[:, channels:], ((0, 0), (0, LANES - heads)))
    y, block_state, sums, reach, query = mix(raw, steps, conv_w, rate, skip, level_w, count)
    level_wt = level_w.reshape(-1).astype(F32) / 256.0
    position = lax.axis_index("seq")
    wide = lambda value: jnp.repeat(value, HEAD)[None, :]
    block_state = block_state.astype(F32)
    block_total = sums[0, :heads]
    cross_state = jnp.zeros_like(block_state)
    passed = jnp.zeros_like(block_total)
    local_bits = (count // Q).bit_length() - 1
    for level in range(nseq.bit_length() - 1):
        other_state = swapped(block_state.astype(BF16), "seq", level).astype(F32)
        other_total = swapped(block_total, "seq", level)
        upper = (jnp.right_shift(position, level) & 1).astype(F32)
        weight = upper * level_wt[local_bits + level + 1]
        cross_state = cross_state + weight * wide(jnp.exp(passed)) * other_state
        passed = passed + upper * other_total
        block_state = jnp.where(
            upper > 0.5,
            other_state * wide(jnp.exp(block_total)) + block_state,
            block_state * wide(jnp.exp(other_total)) + other_state,
        )
        block_total = block_total + other_total
    out = finish(live, y, cross_state.astype(BF16), reach, query)
    return out.reshape(1, count, inner)


def solution(mesh):
    in_specs = (P("dp", "seq", None), P(("seq", "dp"), None), P(), P(), P(), P("dp", None), P("dp"))
    out_specs = P("dp", "seq", None)
    return jax.shard_map(body, mesh=mesh, in_specs=in_specs, out_specs=out_specs, check_vma=False)
```

```python
import functools

import jax
import jax.numpy as jnp
from jax import lax
from jax.experimental import pallas as pl
from jax.experimental.pallas import tpu as pltpu
from jax.sharding import PartitionSpec as P

STATE = 128
Q = 64
RIM = 16
LANES = 128
WIDE = 512
TURNED = 3
HEAD = 64
MESH = pl.DeviceIdType.MESH
F32 = jnp.float32
BF16 = jnp.bfloat16


def dot(a, b):
    return jnp.dot(a, b, preferred_element_type=F32)


def chunk_list(inner, padded):
    chunks = [(inner, padded - inner)]
    at = 0
    while at < inner:
        width = WIDE // 2 if inner - at <= WIDE // 2 or len(chunks) == TURNED else WIDE
        chunks.append((at, width))
        at += width
    return chunks


def split_terms(value, terms):
    parts = []
    for _ in range(terms):
        part = value.astype(BF16)
        parts.append(part)
        value = value - part.astype(F32)
    return parts


def expand(value, first, width, terms=2):
    head = lax.broadcasted_iota(jnp.int32, (LANES, width), 0)
    lane = lax.broadcasted_iota(jnp.int32, (LANES, width), 1)
    one = jnp.where(head == first + lane // HEAD, 1.0, 0.0).astype(BF16)
    return dot(jnp.concatenate(split_terms(value, terms), 1), jnp.concatenate([one] * terms, 0))


def convolve(padded_ref, conv_ref, count):
    total = jnp.zeros((count, padded_ref.shape[1]), F32)
    for tap in range(4):
        total = total + padded_ref[pl.ds(RIM - 3 + tap, count), :] * conv_ref[tap : tap + 1, :]
    return total


def causal_mask():
    row = lax.broadcasted_iota(jnp.int32, (LANES, LANES), 0)
    col = lax.broadcasted_iota(jnp.int32, (LANES, LANES), 1)
    return (col <= row) & (row // Q == col // Q)


def prepare(level, padded_bc, steps, conv_bc, rate, query_ref, sums_ref, reach_ref, local):
    keys_t, cumul_s, cumul_t, scores_s, ends_s, steps_s, totals_s = local
    count = query_ref.shape[0]
    both = convolve(padded_bc, conv_bc, count)
    keys = both[:, :STATE].astype(BF16)
    query = both[:, STATE:].astype(BF16)
    query_ref[...] = query
    steps = jnp.maximum(steps, 0.0) + jnp.log1p(jnp.exp(-jnp.abs(steps)))
    steps_s[...] = steps
    decay = -steps * rate
    ones = jnp.where(causal_mask(), 1.0, 0.0).astype(BF16)
    before = jnp.zeros((1, LANES), F32)
    totals_s[...] = jnp.zeros_like(totals_s)
    for p in range(count // LANES):
        rows = slice(p * LANES, (p + 1) * LANES)
        terms = split_terms(decay[rows], 3)
        cumul = dot(ones, terms[2]) + dot(ones, terms[1]) + dot(ones, terms[0])
        cumul_s[rows, :] = cumul
        cumul_t[:, rows] = cumul.T
        keys_p = keys[rows].astype(F32).T.astype(BF16)
        keys_t[:, rows] = keys_p
        scores_s[rows, :] = dot(query[rows], keys_p) * level(0)
        for half in range(2):
            part = cumul[half * Q : (half + 1) * Q]
            total = part[Q - 1 : Q]
            at = slice(p * LANES + half * Q, p * LANES + (half + 1) * Q)
            ends_s[at, :] = jnp.exp(total - part)
            reach_ref[at, :] = jnp.exp(part + before)
            totals_s[2 * p + half : 2 * p + half + 1, :] = total
            before = before + total
    sums_ref[...] = jnp.broadcast_to(before, sums_ref.shape)


def mix_chunk(level, first, padded_s, conv_ref, skip, y_ref, query_ref, local):
    keys_t, cumul_s, cumul_t, scores_s, ends_s, steps_s, totals_s = local
    count, width = y_ref.shape
    stretches = count // Q
    pairs = count // LANES
    causal = causal_mask()
    convolved = convolve(padded_s, conv_ref, count)
    values = (convolved / (1.0 + jnp.exp(-convolved))).astype(BF16).astype(F32)
    driven = (values * expand(steps_s[...], first, width, 3)).astype(BF16)
    ended = (driven.astype(F32) * expand(ends_s[...], first, width)).astype(BF16)
    totals = expand(totals_s[...], first, width, 3)
    heads = width // HEAD
    turn = (LANES - first) % LANES
    left = lax.broadcasted_iota(jnp.int32, (LANES, LANES), 1) < HEAD
    upper = lax.broadcasted_iota(jnp.int32, (LANES, width), 0) < Q
    if not isinstance(first, int):
        first = pl.multiple_of(first, heads)
    states = []
    for p in range(pairs):
        rows = slice(p * LANES, (p + 1) * LANES)
        down = pltpu.roll(cumul_s[rows, :], turn, 1)
        along = cumul_t[pl.ds(first, heads), rows]
        scores = scores_s[rows, :]
        for two in range(heads // 2):
            cols = slice(two * LANES, (two + 1) * LANES)
            parts = []
            for h in (2 * two, 2 * two + 1):
                differ = down[:, h : h + 1] - along[h : h + 1, :]
                weight = jnp.exp(jnp.where(causal, differ, -1e30)) * scores
                parts.append(dot(weight.astype(BF16), driven[rows, cols]))
            y_ref[rows, cols] = (
                jnp.where(left, parts[0], parts[1]) + skip[:, cols] * values[rows, cols]
            )
        ended_p = ended[rows]
        keys_p = keys_t[:, rows]
        zero = jnp.zeros_like(ended_p)
        states.append(dot(keys_p, jnp.where(upper, ended_p, zero)))
        states.append(dot(keys_p, jnp.where(upper, zero, ended_p)))

    sums = [totals[i : i + 1] for i in range(stretches)]
    carried = [None] * stretches
    blocks, block_sums = states, sums
    for bit in range(stretches.bit_length() - 1):
        weight = level(bit + 1)
        for k in range(1, len(blocks), 2):
            passed = jnp.zeros((1, width), F32)
            for j in range(k << bit, (k + 1) << bit):
                term = blocks[k - 1] * (weight * jnp.exp(passed))
                carried[j] = term if carried[j] is None else carried[j] + term
                passed = passed + sums[j]
        merged = [
            blocks[k] * jnp.exp(block_sums[k + 1]) + blocks[k + 1] for k in range(0, len(blocks), 2)
        ]
        block_sums = [block_sums[k] + block_sums[k + 1] for k in range(0, len(blocks), 2)]
        blocks = merged
    grown = expand(jnp.exp(cumul_s[...]), first, width)
    for j in range(1, stretches):
        rows = slice(j * Q, (j + 1) * Q)
        y_ref[rows, :] += grown[rows] * dot(query_ref[rows, :], carried[j].astype(BF16))
    return blocks[0]


def finish_chunk(first, live_to, y, cross, reach_ref, query_ref, out_ref):
    count, width = out_ref.shape
    output = y + expand(reach_ref[...], first, width) * dot(query_ref[...], cross)
    squares = output * output
    row = lax.broadcasted_iota(jnp.int32, (LANES, LANES), 0)
    col = lax.broadcasted_iota(jnp.int32, (LANES, LANES), 1)
    same = jnp.where(row // HEAD == col // HEAD, 1.0 / HEAD, 0.0).astype(BF16)
    same = jnp.concatenate([same, same], 0)
    live = lax.broadcasted_iota(jnp.int32, (count, LANES), 0) < live_to
    for two in range(width // LANES):
        cols = slice(two * LANES, (two + 1) * LANES)
        mean = dot(jnp.concatenate(split_terms(squares[:, cols], 2), 1), same)
        out_ref[:, cols] = jnp.where(live, output[:, cols] * lax.rsqrt(mean + 1e-05), 0.0).astype(BF16)


def local_scratch(count):
    return [
        pltpu.VMEM((STATE, count), BF16),
        pltpu.VMEM((count, LANES), F32),
        pltpu.VMEM((LANES, count), F32),
        pltpu.VMEM((count, LANES), F32),
        pltpu.VMEM((count, LANES), F32),
        pltpu.VMEM((count, LANES), F32),
        pltpu.VMEM((max(8, count // Q), LANES), F32),
    ]


def mix_kernel(
    level_ref, raw_ref, bc_ref, step_ref, conv_ref, conv_bc_ref, rate_ref, skip_ref,
    y_ref, state_ref, sums_ref, reach_ref, query_ref, padded_s, padded_bc, *local,
):
    chunk = pl.program_id(0)
    level = lambda at: level_ref[0, at].astype(F32) / 256.0

    @pl.when(chunk == 0)
    def _():
        padded_bc[...] = bc_ref[...].astype(F32)
        steps = step_ref[pl.ds(RIM, y_ref.shape[0]), :]
        prepare(level, padded_bc, steps, conv_bc_ref, rate_ref[...], query_ref, sums_ref, reach_ref, local)

    padded_s[...] = raw_ref[...].astype(F32)
    first = chunk * (WIDE // HEAD)
    state = mix_chunk(level, first, padded_s, conv_ref, skip_ref[...], y_ref, query_ref, local)
    state_ref[...] = state.astype(BF16)


def mix(raw, steps, conv_w, rate, skip, level_w, count):
    inner = conv_w.shape[1] - 2 * STATE
    total = raw.shape[0]
    whole = lambda shape: pl.BlockSpec(shape, lambda i: (0, 0))
    part = lambda rows: pl.BlockSpec((rows, WIDE), lambda i: (0, i))
    tail = lambda rows: pl.BlockSpec((rows, 2 * STATE), lambda i: (0, inner // (2 * STATE)))
    return pl.pallas_call(
        mix_kernel,
        grid=(inner // WIDE,),
        in_specs=[
            pl.BlockSpec(memory_space=pltpu.SMEM),
            part(total),
            tail(total),
            whole((total, LANES)),
            part(4),
            tail(4),
            whole((1, LANES)),
            part(1),
        ],
        out_specs=(part(count), part(STATE), whole((8, LANES)), whole((count, LANES)), whole((count, STATE))),
        out_shape=(
            jax.ShapeDtypeStruct((count, inner), F32),
            jax.ShapeDtypeStruct((STATE, inner), BF16),
            jax.ShapeDtypeStruct((8, LANES), F32),
            jax.ShapeDtypeStruct((count, LANES), F32),
            jax.ShapeDtypeStruct((count, STATE), BF16),
        ),
        scratch_shapes=[
            pltpu.VMEM((total, WIDE), F32),
            pltpu.VMEM((total, 2 * STATE), F32),
        ]
        + local_scratch(count),
        compiler_params=pltpu.CompilerParams(vmem_limit_bytes=48 * 2**20),
        name="mix",
    )(level_w, raw, raw, steps, conv_w, conv_w, rate, skip)


def finish_kernel(live_ref, y_ref, cross_ref, reach_ref, query_ref, out_ref):
    first = pl.program_id(0) * (WIDE // HEAD)
    finish_chunk(first, live_ref[0], y_ref[...], cross_ref[...], reach_ref, query_ref, out_ref)


def finish(live, y, cross, reach, query):
    count, inner = y.shape
    whole = lambda shape: pl.BlockSpec(shape, lambda i: (0, 0))
    part = lambda rows: pl.BlockSpec((rows, WIDE), lambda i: (0, i))
    return pl.pallas_call(
        finish_kernel,
        grid=(inner // WIDE,),
        in_specs=[
            pl.BlockSpec(memory_space=pltpu.SMEM),
            part(count),
            part(STATE),
            whole((count, LANES)),
            whole((count, STATE)),
        ],
        out_specs=part(count),
        out_shape=jax.ShapeDtypeStruct((count, inner), BF16),
        compiler_params=pltpu.CompilerParams(vmem_limit_bytes=48 * 2**20),
        name="finish",
    )(live, y, cross, reach, query)


def swapped(value, axis, stride):
    mask = 2**stride
    pairs = [(source, source ^ mask) for source in range(lax.axis_size(axis))]
    return lax.ppermute(value, axis, pairs)


def fused_kernel(
    nz, n, inner, level_ref, live_ref, tok_ref, w_ref, conv_ref, rate_ref, skip_ref, out_ref,
    ext, wbuf, tok_sem, rim_sem, own_sem, send_sem, recv_sem, core_send, core_recv,
    y_s, out_s, padded_s, query_s, reach_s, sums_s, all_sums, own_state, pair_in, pair_state, quad_in,
    quad_state, third_in, cross_s, sum_send, sum_recv, state_send, state_recv, out_sem, rates_s, skip_wide, sums_wide, *local,
):
    seq = lax.axis_index("seq")
    dp = lax.axis_index("dp")
    nseq = nz * n
    z, x = seq // n, seq % n
    y, core = dp // 2, dp % 2
    rows = w_ref.shape[0]
    count = tok_ref.shape[0]
    padded = w_ref.shape[1]
    chunks = chunk_list(inner, padded)
    after = (seq + 1) % nseq
    prior = (seq + nseq - 1) % nseq

    def place(dz, da, db):
        dx = da * (1 - core) + db * core
        dy = da * core + db * (1 - core)
        return ((z + dz) % nz) * n + (x + dx) % n, ((y + dy) % n) * 2 + core

    def rows_of(device):
        at = device[0] * (2 * n) + device[1]
        return pl.ds(pl.multiple_of(at * rows, rows), rows)

    offsets = [(dz, da, db) for dz in range(nz) for da in range(n) for db in range(n)]
    other = (seq, y * 2 + 1 - core)
    along_seq = [((seq + by) % nseq, dp) for by in range(1, nseq)]

    barrier = pltpu.get_barrier_semaphore()
    greeted = along_seq + [(seq, ((y + by) % n) * 2 + core) for by in range(1, n)] + [other]
    for device in greeted:
        pl.semaphore_signal(barrier, inc=1, device_id=device, device_id_type=MESH)
    pl.semaphore_wait(barrier, len(greeted))

    rim = pltpu.make_async_remote_copy(
        src_ref=tok_ref.at[pl.ds(count - RIM, RIM)],
        dst_ref=ext.at[pl.ds(0, RIM)],
        send_sem=rim_sem.at[0],
        recv_sem=rim_sem.at[1],
        device_id=(after, dp),
        device_id_type=MESH,
    )
    own_rows = rows_of((seq, dp))
    number = {offset: at for at, offset in enumerate(offsets)}
    sends = []

    def link_copy(c, offset, step):
        at, width = chunks[c]
        cols = pl.ds(at, width)
        where = rows_of(place(*offset))
        mine = offset == (0, 0, 0)
        lands = tuple((o - s) % m for o, s, m in zip(offset, step, (nz, n, n)))
        slot = number[lands]
        return pltpu.make_async_remote_copy(
            src_ref=w_ref.at[:, cols] if mine else wbuf.at[where, cols],
            dst_ref=wbuf.at[where, cols],
            send_sem=send_sem.at[c, slot],
            recv_sem=recv_sem.at[c, slot],
            device_id=place(*step),
            device_id_type=MESH,
        )

    def arrived(c, offset):
        at, width = chunks[c]
        ref = wbuf.at[rows_of(place(*offset)), pl.ds(at, width)]
        pltpu.make_async_copy(ref, ref, recv_sem.at[c, number[offset]]).wait()

    def core_copy(c, offset):
        at, width = chunks[c]
        cols = pl.ds(at, width)
        where = rows_of(place(*offset))
        mine = offset == (0, 0, 0)
        return pltpu.make_async_remote_copy(
            src_ref=w_ref.at[:, cols] if mine else wbuf.at[where, cols],
            dst_ref=wbuf.at[where, cols],
            send_sem=core_send.at[c, number[offset]],
            recv_sem=core_recv.at[c, number[offset]],
            device_id=other,
            device_id_type=MESH,
        )

    def core_arrived(c, offset):
        dz, da, db = offset
        at, width = chunks[c]
        theirs = 1 - core
        dx = da * (1 - theirs) + db * theirs
        dy = da * theirs + db * (1 - theirs)
        device = ((z + dz) % nz) * n + (x + dx) % n, ((y + dy) % n) * 2 + theirs
        ref = wbuf.at[rows_of(device), pl.ds(at, width)]
        pltpu.make_async_copy(ref, ref, core_recv.at[c, number[offset]]).wait()

    def start(copy):
        copy.start()
        sends.append(copy)

    sizes = (nz, n, n)

    def order_of(c):
        return (1, 2, 0) if c == TURNED else (0, 1, 2)

    def stage_of(c, offset):
        return max([at for at, axis in enumerate(order_of(c)) if offset[axis]], default=-1)

    def send_on(c, offset):
        for axis in order_of(c)[stage_of(c, offset) + 1 :]:
            for by in range(1, sizes[axis]):
                start(link_copy(c, offset, tuple(by if axis == at else 0 for at in range(3))))
        start(core_copy(c, offset))

    def send_own(c):
        send_on(c, (0, 0, 0))

    def forward(c, stage):
        for offset in offsets[1:]:
            if stage_of(c, offset) == stage:
                arrived(c, offset)
                send_on(c, offset)

    level = lambda at: level_ref[0, at].astype(F32) / 256.0
    bits = (count // Q).bit_length() - 1

    def sum_copy(by):
        return pltpu.make_async_remote_copy(
            src_ref=sums_s,
            dst_ref=all_sums.at[seq],
            send_sem=sum_send.at[by],
            recv_sem=sum_recv.at[by],
            device_id=((seq + by) % nseq, dp),
            device_id_type=MESH,
        )

    def multiply(c):
        for offset in offsets:
            core_arrived(c, offset)
        at, width = chunks[c]
        if c == 0:
            mid = at + 2 * STATE
            padded_s[:, 0 : 2 * STATE] = dot(ext[...], wbuf[:, at:mid]).astype(BF16).astype(F32)
            steps = dot(ext[...], wbuf[:, mid:])[RIM:]
            conv_bc = conv_ref.at[:, at:mid]
            prepare(
                level, padded_s.at[:, 0 : 2 * STATE], steps, conv_bc, rates_s[0:1],
                query_s, sums_s, reach_s, local,
            )
            all_sums[seq] = sums_s[...]
            for by in range(1, nseq):
                sum_copy(by).start()
            return

        @pl.loop(0, width // 256)
        def _(tile):
            cols = pl.ds(pl.multiple_of(at + tile * 256, 256), 256)
            lands = pl.ds(pl.multiple_of(tile * 256, 256), 256)
            padded_s[:, lands] = dot(ext[...], wbuf[:, cols]).astype(BF16).astype(F32)

        cols = pl.ds(at, width)
        state = mix_chunk(
            level, at // HEAD, padded_s.at[:, 0:width], conv_ref.at[:, cols], skip_wide[1:2, cols],
            y_s.at[:, cols], query_s, local,
        )
        own_state[:, cols] = state.astype(BF16)
        state_copy(c, 0).start()

    def state_copy(c, hop):
        at, width = chunks[c]
        cols = pl.ds(at, width)
        source, target, device = (
            (own_state, pair_in, (seq + 1 - 2 * x, dp)),
            (pair_state, quad_in, ((seq + n) % nseq, dp)),
            (quad_state, quad_in, ((seq + n) % nseq, dp)),
            (quad_in, third_in, ((seq + n) % nseq, dp)),
        )[hop]
        return pltpu.make_async_remote_copy(
            src_ref=source.at[:, cols],
            dst_ref=target.at[:, cols],
            send_sem=state_send.at[c, hop],
            recv_sem=state_recv.at[c, hop],
            device_id=device,
            device_id_type=MESH,
        )

    def sums_of(c, device):
        at, width = chunks[c]
        return sums_wide[pl.ds(device, 1), pl.ds(at, width)]

    upper = x.astype(F32)
    odd = z % 2

    def passed_pair(c):
        return upper * sums_of(c, z * n)

    def exchange(c, stage):
        at, width = chunks[c]
        cols = pl.ds(at, width)
        if stage == 0:
            state_copy(c, 0).wait_recv()
            mine = own_state[:, cols].astype(F32)
            theirs = pair_in[:, cols].astype(F32)
            cross_s[:, cols] = theirs * (upper * level(bits + 1))
            first = jnp.where(x == 0, mine, theirs)
            second = jnp.where(x == 0, theirs, mine)
            pair = first * jnp.exp(sums_of(c, z * n + 1)) + second
            pair_state[:, cols] = pair.astype(BF16)

            @pl.when(odd == 0)
            def _():
                state_copy(c, 1).start()

        elif stage == 1:

            @pl.when(odd == 1)
            def _():
                state_copy(c, 1).wait_recv()
                lower = quad_in[:, cols].astype(F32)
                cross_s[:, cols] += lower * (level(bits + 2) * jnp.exp(passed_pair(c)))
                pair_sum = sums_of(c, z * n) + sums_of(c, z * n + 1)
                quad = lower * jnp.exp(pair_sum) + pair_state[:, cols].astype(F32)
                quad_state[:, cols] = quad.astype(BF16)

            @pl.when(z == 1)
            def _():
                state_copy(c, 2).start()

        else:

            @pl.when(z == 2)
            def _():
                state_copy(c, 2).wait_recv()
                state_copy(c, 3).start()
                lower = quad_in[:, cols].astype(F32)
                cross_s[:, cols] += lower * (level(bits + 3) * jnp.exp(passed_pair(c)))

            @pl.when(z == 3)
            def _():
                state_copy(c, 3).wait_recv()
                lower = third_in[:, cols].astype(F32)
                before = passed_pair(c) + sums_of(c, z * n - 1) + sums_of(c, z * n - 2)
                cross_s[:, cols] += lower * (level(bits + 3) * jnp.exp(before))

            view = out_s.at[:, cols]
            finish_chunk(
                at // HEAD, live_ref[0], y_s[:, cols], cross_s[:, cols].astype(BF16), reach_s, query_s, view
            )
            out_copy(c).start()

    def out_copy(c):
        at, width = chunks[c]
        cols = pl.ds(at, width)
        return pltpu.make_async_copy(out_s.at[:, cols], out_ref.at[:, cols], out_sem.at[c])

    send_own(0)
    rim.start()
    tokens_in = pltpu.make_async_copy(tok_ref, ext.at[pl.ds(RIM, count)], tok_sem.at[0])
    tokens_in.start()
    own_in = pltpu.make_async_copy(w_ref, wbuf.at[own_rows], own_sem.at[0])
    own_in.start()
    send_own(1)
    send_own(2)
    rates_s[...] = jnp.zeros_like(rates_s)
    rates_s[0:1, 0 : rate_ref.shape[1]] = rate_ref[...]
    rates_s[1:2, 0 : rate_ref.shape[1]] = skip_ref[...]
    skip_wide[...] = expand(rates_s[...], 0, inner, 3)

    last = len(chunks) - 1
    for step in range(last + 7):
        if step <= last:
            forward(step, 0)
        if step + 3 <= last:
            send_own(step + 3)
        if 0 <= step - 1 <= last:
            forward(step - 1, 1)
        if step == 3:
            rim.wait()
            tokens_in.wait()
            own_in.wait()

            @pl.when(seq == 0)
            def _():
                ext[0:RIM, :] = jnp.zeros((RIM, ext.shape[1]), BF16)

        if 0 <= step - 3 <= last:
            multiply(step - 3)
        for stage in (0, 1, 2):
            if 1 <= step - 4 - stage <= last:
                if step - 4 - stage == 1 and stage == 0:
                    for by in range(1, nseq):
                        sum_copy(by).wait_recv()
                    row = lax.broadcasted_iota(jnp.int32, (8, LANES), 0)
                    packed = jnp.zeros((8, LANES), F32)
                    for device in range(nseq):
                        packed = jnp.where(row == device, all_sums[device], packed)
                    sums_wide[...] = expand(packed, 0, inner, 3)
                exchange(step - 4 - stage, stage)
        if 0 <= step - 2 <= last:
            forward(step - 2, 2)
    for copy in sends:
        copy.wait_send()
    for by in range(1, nseq):
        sum_copy(by).wait_send()
    for c in range(1, last + 1):
        out_copy(c).wait()
        state_copy(c, 0).wait_send()

        @pl.when(odd == 0)
        def _():
            state_copy(c, 1).wait_send()

        @pl.when(z == 1)
        def _():
            state_copy(c, 2).wait_send()

        @pl.when(z == 2)
        def _():
            state_copy(c, 3).wait_send()


def fused(tokens, w_in, conv_w, rate, skip, level_w, live, nseq, ndp):
    count, depth = tokens.shape
    padded = -(-w_in.shape[1] // LANES) * LANES
    w_in = jnp.pad(w_in, ((0, 0), (0, padded - w_in.shape[1])))
    inner = conv_w.shape[1] - 2 * STATE
    n = ndp // 2
    nz = nseq // n
    total = count + RIM
    shards = nz * n * n
    chunks = len(chunk_list(inner, padded))
    smem = pl.BlockSpec(memory_space=pltpu.SMEM)
    vmem = pl.BlockSpec(memory_space=pltpu.VMEM)
    anywhere = pl.BlockSpec(memory_space=pl.ANY)
    state = pltpu.VMEM((STATE, inner), BF16)
    return pl.pallas_call(
        functools.partial(fused_kernel, nz, n, inner),
        out_shape=jax.ShapeDtypeStruct((count, inner), BF16),
        in_specs=[smem, smem, anywhere, anywhere, vmem, vmem, vmem],
        out_specs=anywhere,
        scratch_shapes=[
            pltpu.VMEM((total, depth), BF16),
            pltpu.VMEM((depth, padded), BF16),
            pltpu.SemaphoreType.DMA((1,)),
            pltpu.SemaphoreType.DMA((2,)),
            pltpu.SemaphoreType.DMA((1,)),
        ]
        + [pltpu.SemaphoreType.DMA((chunks, shards))] * 4
        + [
            pltpu.VMEM((count, inner), F32),
            pltpu.VMEM((count, inner), BF16),
            pltpu.VMEM((total, WIDE), F32),
            pltpu.VMEM((count, STATE), BF16),
            pltpu.VMEM((count, LANES), F32),
            pltpu.VMEM((8, LANES), F32),
            pltpu.VMEM((nseq, 8, LANES), F32),
        ]
        + [state] * 6
        + [
            pltpu.VMEM((STATE, inner), F32),
            pltpu.SemaphoreType.DMA((nseq,)),
            pltpu.SemaphoreType.DMA((nseq,)),
            pltpu.SemaphoreType.DMA((chunks, 4)),
            pltpu.SemaphoreType.DMA((chunks, 4)),
            pltpu.SemaphoreType.DMA((chunks,)),
            pltpu.VMEM((8, LANES), F32),
            pltpu.VMEM((8, inner), F32),
            pltpu.VMEM((8, inner), F32),
        ]
        + local_scratch(count),
        compiler_params=pltpu.CompilerParams(
            collective_id=0, has_side_effects=True, vmem_limit_bytes=60 * 2**20
        ),
        name="fused",
    )(level_w, live, tokens, w_in, conv_w, rate, skip)


def body(tokens, w_in, conv_w, a_rate, d_skip, level_w, lengths):
    token_rows = tokens.reshape(-1, tokens.shape[-1])
    count = token_rows.shape[0]
    heads = a_rate.shape[0]
    inner = conv_w.shape[1] - 2 * STATE
    nseq = lax.axis_size("seq")
    live = lengths - lax.axis_index("seq") * count
    ndp = lax.axis_size("dp")
    if (nseq, ndp) == (8, 4):
        out = fused(token_rows, w_in, conv_w, a_rate[None, :], d_skip[None, :], level_w, live, nseq, ndp)
        return out.reshape(1, count, inner)
    rate = jnp.pad(a_rate[None, :], ((0, 0), (0, LANES - heads)))
    skip = jnp.repeat(d_skip, HEAD)[None, :]
    channels = conv_w.shape[1]
    edge = lax.ppermute(token_rows[count - RIM :], "seq", [(i, i + 1) for i in range(nseq - 1)])
    full = lax.all_gather(w_in, ("seq", "dp"), axis=0, tiled=True)
    projected = dot(jnp.concatenate([edge, token_rows], 0), full)
    raw = projected[:, :channels].astype(BF16)
    steps = jnp.pad(projected[:, channels:], ((0, 0), (0, LANES - heads)))
    y, block_state, sums, reach, query = mix(raw, steps, conv_w, rate, skip, level_w, count)
    level_wt = level_w.reshape(-1).astype(F32) / 256.0
    position = lax.axis_index("seq")
    wide = lambda value: jnp.repeat(value, HEAD)[None, :]
    block_state = block_state.astype(F32)
    block_total = sums[0, :heads]
    cross_state = jnp.zeros_like(block_state)
    passed = jnp.zeros_like(block_total)
    local_bits = (count // Q).bit_length() - 1
    for level in range(nseq.bit_length() - 1):
        other_state = swapped(block_state.astype(BF16), "seq", level).astype(F32)
        other_total = swapped(block_total, "seq", level)
        upper = (jnp.right_shift(position, level) & 1).astype(F32)
        weight = upper * level_wt[local_bits + level + 1]
        cross_state = cross_state + weight * wide(jnp.exp(passed)) * other_state
        passed = passed + upper * other_total
        block_state = jnp.where(
            upper > 0.5,
            other_state * wide(jnp.exp(block_total)) + block_state,
            block_state * wide(jnp.exp(other_total)) + other_state,
        )
        block_total = block_total + other_total
    out = finish(live, y, cross_state.astype(BF16), reach, query)
    return out.reshape(1, count, inner)


def solution(mesh):
    in_specs = (P("dp", "seq", None), P(("seq", "dp"), None), P(), P(), P(), P("dp", None), P("dp"))
    out_specs = P("dp", "seq", None)
    return jax.shard_map(body, mesh=mesh, in_specs=in_specs, out_specs=out_specs, check_vma=False)
```
